256 devices in a mesh: rows: 64 (over z, x, core), cols: 4 (over y).
Axes of the slice: x: 4, y: 4, z: 8, core: 2. Of those that a mesh axis runs over, the one named last changes fastest.
Arguments:
- matrix_t: float32 [256, 524288], P('cols', 'rows'), may hold values from -6 to 6
- signs: int32 [524288], P('rows'), may hold values from -1 to 1, as said below
- sample_ids: int32 [16384], P('rows'), may hold values from 0 to 524287, as said below
Outputs:
- sketch: float32 [256, 16384], P('cols', 'rows')
- gram: float32 [256, 256], P('cols')
The draws below stay inside these ranges and needn't reach their ends.
Inputs may be any that keep to these rules, and one draw needn't show every extreme that they name: `sample_ids`: sketch rows come in 64 owner blocks of 256; inside owner block o, positions s * 4 to (s + 1) * 4 - 1 name rows of row block s (rows s * 8192 to (s + 1) * 8192 - 1); no row is named twice. The ids may cross between devices in any lossless encoding, several packed into one 32-bit word. `signs`: each entry is -1 or 1.
All inputs are finite; a program needn't handle non-finite values.
Results may differ from the reference program's by a relative error of at most 0.00013.
Values sent between devices are 32-bit elements; how exact they have to be, the bound alone decides.
A program may use at most 64 MiB of HBM per device.

```python
import jax
import jax.numpy as jnp
from jax import lax

WIN = 256
ROWS_DEV = 8192
SAMP_PAIR = 4
MROWS = 524288
SAMPLES = 16384
N_ROWS = 64


def draw_signs(key, part):
    key = jax.random.fold_in(key, 11)
    bits = jax.random.randint(key, (MROWS,), 0, 2, dtype=jnp.int32)
    return 2 * bits - 1


def draw_sample_ids(key, part):
    key = jax.random.fold_in(key, 23)
    keys = jax.random.split(key, N_ROWS)
    take = N_ROWS * SAMP_PAIR

    def pick(one_key):
        return jax.random.permutation(one_key, ROWS_DEV)[:take].astype(jnp.int32)
    chosen = jax.vmap(pick)(keys)
    chosen = chosen.reshape(N_ROWS, N_ROWS, SAMP_PAIR)
    base = (jnp.arange(N_ROWS, dtype=jnp.int32) * ROWS_DEV)[:, None, None]
    owners = jnp.transpose(chosen + base, (1, 0, 2))
    return owners.reshape(SAMPLES)


def block_scale(stream_key, dims, shards, low, top_value):
    loudness, own = 1.0, jax.random.fold_in(stream_key, 6)
    for axis_at, shards_of in shards:
        steps = jnp.exp(jax.random.uniform(jax.random.fold_in(own, axis_at), (shards_of,), jnp.float32, low / len(shards), top_value / len(shards)))
        loudness = loudness * jnp.repeat(steps, dims[axis_at] // shards_of).reshape([-1 if axis == axis_at else 1 for axis in range(len(dims))])
    return loudness


def gaussian(key, shape, scale, most, shards=(), kind=jnp.bfloat16):
    factor_of = block_scale(key, shape, shards, -0.22, 0.18) if shards else 1.0
    result = jax.random.normal(key, shape, jnp.float32) * scale * factor_of
    return jnp.minimum(jnp.maximum(result, -most), most).astype(kind)


def setup_inputs(seed: int = 0) -> dict:
    seeds = jax.random.split(jax.random.key(seed), 4)
    matrix_t = gaussian(seeds[0], (WIN, MROWS), 1.0, 6.0, ((0, 4), (1, 64)), jnp.float32)
    signs = draw_signs(jax.random.fold_in(seeds[3], 71), 0)
    sample_ids = draw_sample_ids(jax.random.fold_in(seeds[3], 71), 0)
    return {"matrix_t": matrix_t, "signs": signs, "sample_ids": sample_ids}


def sylvester(order):
    index = jnp.arange(order, dtype=jnp.int32)
    parity = jnp.zeros((order, order), jnp.int32)
    width = max(order.bit_length() - 1, 0)
    for bit in range(width):
        parity = parity + ((index[:, None] >> bit) & 1) * ((index[None, :] >> bit) & 1)
    return (1 - 2 * (parity % 2)).astype(jnp.float32)


def reference(matrix_t, signs, sample_ids):
    total = matrix_t.shape[1]
    signed = matrix_t * signs.astype(jnp.float32)[None, :]
    inner = ROWS_DEV // 128
    blocks = signed.reshape(WIN, N_ROWS, 128, inner)
    high = lax.Precision.HIGHEST
    blocks = jnp.einsum("st,ctaq->csaq", sylvester(N_ROWS), blocks, precision=high)
    blocks = jnp.einsum("ab,csbq->csaq", sylvester(128), blocks, precision=high)
    blocks = jnp.einsum("pq,csaq->csap", sylvester(inner), blocks, precision=high)
    transformed = blocks.reshape(WIN, total) * (1.0 / (total ** 0.5))
    sketch = jnp.take(transformed, sample_ids.astype(jnp.int32), axis=1)
    gram = jnp.dot(sketch, sketch.T, precision=high, preferred_element_type=jnp.float32) / SAMPLES
    return sketch, gram
```

```python
import jax
import jax.numpy as jnp
from jax import lax
from jax.experimental import pallas as pl
from jax.experimental.pallas import tpu as pltpu
from jax.sharding import PartitionSpec as P

MESH = pl.DeviceIdType.MESH
F32, BF16, I32 = jnp.float32, jnp.bfloat16, jnp.int32

NX, NZ, NY = 4, 8, 4
CHIPS = NX * NZ
COLS, ROWS = 64, 8192
KEEP = 4
LIST = CHIPS * KEEP
RA = 80
HA = RA // 2
RB = LIST - RA
HB = RB // 2
GA, GB = 4, 2
PA, PB = NZ // GA, NX // GB
UA, UB = 20, 24


def hadamard_rows(copies):
    shape = (128, 128 * copies)
    parity = lax.broadcasted_iota(I32, shape, 0) & lax.broadcasted_iota(I32, shape, 1) & 127
    for shift in (4, 2, 1):
        parity = parity ^ (parity >> shift)
    return (1 - 2 * (parity & 1)).astype(F32).astype(BF16)


def butterflies(parts):
    for stride in (1, 2, 4):
        done = list(parts)
        for i in range(8):
            if not i & stride:
                done[i] = parts[i] + parts[i | stride]
                done[i | stride] = parts[i] - parts[i | stride]
        parts = done
    return parts


def kernel(
    m_ref, s_ref, id_ref, sk_ref, g_ref,
    x_v, xp_v, sp_v, y_v, t_v, idp_v, ids_v, ids_s, sg_v,
    a1s, a1r, a2s, a2r, a_sum, azr,
    b1s, b1r, b2s, b2r, b_sum, bxr,
    f_v, fp_v, p_v, g1r, g2r, g3r,
    lx_sem, sm_sem, xs_sem, xr_sem, ps_sem, pr_sem, is_sem, ir_sem, rs_sem, rr_sem,
    gs_sem, gr_sem,
):
    me, y = lax.axis_index("rows"), lax.axis_index("cols")
    core, chip = me % 2, me // 2
    x, z = chip % NX, chip // NX
    corner = x * 2 + core

    def at(x_to, z_to, core_to):
        return {"rows": (lax.rem(z_to + NZ, NZ) * NX + lax.rem(x_to + NX, NX)) * 2 + core_to}

    partner = at(x, z, 1 - core)

    def remote(src, dst, send, recv, device):
        return pltpu.make_async_remote_copy(
            src_ref=src, dst_ref=dst, send_sem=send, recv_sem=recv, device_id=device, device_id_type=MESH
        )

    def own_copy(q):
        piece = pl.ds(pl.multiple_of(q * 1024, 1024), 1024)
        return pltpu.make_async_copy(m_ref.at[:, piece], x_v.at[q], lx_sem.at[q])

    for q in range(8):
        own_copy(q).start()

    barrier = pltpu.get_barrier_semaphore()

    def greet(device):
        pl.semaphore_signal(barrier, inc=1, device_id=device, device_id_type=MESH)

    greet(partner)

    def greet_chip(o, _):
        to = lax.rem(chip + o, CHIPS)
        greet({"rows": to * 2 + core})
        return 0

    lax.fori_loop(1, CHIPS, greet_chip, 0)
    for o in range(1, NX):
        greet(at(x + o, z, 1 - core))
    for o in range(1, NY):
        greet({"cols": lax.rem(y + o, NY)})
    pl.semaphore_wait(barrier, 1 + CHIPS - 1 + NX - 1 + NY - 1)

    ids_out = remote(id_ref.at[1 - core], idp_v, ps_sem.at[0], pr_sem.at[0], partner)
    sign_out = remote(s_ref, sp_v, ps_sem.at[1], pr_sem.at[1], partner)
    ids_out.start()
    sign_out.start()

    def pair_copy(q):
        piece = pl.ds(pl.multiple_of(q * 1024, 1024), 1024)
        return remote(m_ref.at[:, piece], xp_v.at[q], xs_sem.at[q], xr_sem.at[q], partner)

    for q in range(8):
        pair_copy(q).start()

    ids_out.wait_recv()
    mine, other = id_ref[core], idp_v[...]
    left = jnp.where(core == 0, mine, other)
    right = jnp.where(core == 0, other, mine)
    ids_v[chip] = left | ((right ^ (ROWS // 2)) << 16)

    def ids_copy(o):
        to = lax.rem(chip + o, CHIPS)
        return remote(ids_v.at[chip], ids_v.at[chip], is_sem, ir_sem, {"rows": to * 2 + core})

    def ids_send(o, _):
        ids_copy(o).start()
        return 0

    lax.fori_loop(1, CHIPS, ids_send, 0)

    block = lax.broadcasted_iota(I32, (LIST, 128), 0) // KEEP
    parity = block & chip
    for shift in (4, 2, 1):
        parity = parity ^ (parity >> shift)
    sg_v[...] = (1 - 2 * (parity & 1)).astype(F32)

    had = hadamard_rows(2)
    flip = (1 - 2 * core).astype(F32)
    sign_out.wait_recv()

    with jax.named_scope("local transform"):

        def chunk(q, _):
            own_copy(q).wait()
            pair_copy(q).wait_recv()
            own_sign = s_ref[pl.ds(pl.multiple_of(q * 8, 8), 8), :].astype(F32) * flip
            far_sign = sp_v[pl.ds(pl.multiple_of(q * 8, 8), 8), :].astype(F32)
            parts = []
            for i in range(8):
                lanes = slice(i * 128, (i + 1) * 128)
                parts.append(x_v[q, :, lanes] * own_sign[i : i + 1] + xp_v[q, :, lanes] * far_sign[i : i + 1])
            parts = butterflies(parts)
            for p in range(4):
                two = jnp.concatenate([parts[2 * p], parts[2 * p + 1]], 0)
                high = two.astype(BF16)
                low = (two - high.astype(F32)).astype(BF16)
                y_v[q, p] = lax.dot_general(
                    had, jnp.concatenate([high, low], 1), (((1,), (1,)), ((), ())), preferred_element_type=F32
                )
            return 0

        lax.fori_loop(0, 8, chunk, 0)

    pltpu.make_async_copy(ids_v.at[pl.ds(0, CHIPS - 1)], ids_v.at[pl.ds(0, CHIPS - 1)], ir_sem).wait()
    lists = pltpu.make_async_copy(ids_v, ids_s, sm_sem)
    lists.start()

    with jax.named_scope("across chunks"):

        def across(i, _):
            p = i // 4
            for t in range(4):
                row = pl.multiple_of((i % 4) * 32 + t * 8, 8)
                parts = butterflies([y_v[q, p, pl.ds(row, 8), :] for q in range(8)])
                for q in range(8):
                    to = pl.multiple_of(q * 512 + p * 128 + row, 8)
                    t_v[pl.ds(to, 8), :] = parts[q]
                    t_v[pl.ds(to + ROWS // 2, 8), :] = pltpu.roll(parts[q], 64, 1)
            return 0

        lax.fori_loop(0, 16, across, 0)
    lists.wait()

    half = lax.broadcasted_iota(I32, (1, 128), 1) < 64

    def gather(dst, chip_of, pieces, first, count, unroll):
        steps = count // unroll

        def step(i, _):
            piece = i // steps
            start = first + (i - piece * steps) * unroll
            of = chip_of(piece)
            got = []
            for u in range(unroll):
                word = ids_s[of, 0, start + u]
                a = t_v[pl.ds(word & 0xFFFF, 1), :]
                b = t_v[pl.ds(word >> 16, 1), :]
                got.append(jnp.where(half, a, b))
            for u in range(unroll):
                dst[pl.ds(i * unroll + u, 1), :] = got[u]
            return 0

        lax.fori_loop(0, pieces * steps, step, 0)

    count = [0]

    def send(src, dst, device):
        n = count[0]
        count[0] += 1
        copy = remote(src, dst, rs_sem.at[n], rr_sem.at[n], device)
        copy.start()
        return copy

    xp, xm = at(x + 1, z, core), at(x - 1, z, core)
    zp, zm = at(x, z + 1, core), at(x, z - 1, core)
    z_order = (4, 3, -3, 2, -2, 1, -1, 0)
    x_order = (2, 1, -1, 0)

    def chip_at(dx, dz):
        return lax.rem(z + dz + NZ, NZ) * NX + lax.rem(x + dx + NX, NX)

    def pick(order, g, width, n):
        value = jnp.int32(order[g * width])
        for k in range(1, width):
            value = jnp.where(n == k, order[g * width + k], value)
        return value

    sent = []

    a1, a2, az = {}, {}, {}

    def a_one(g):
        for d, first, to in ((0, 0, xp), (1, HA, xm)):
            dst = a1s.at[g, d]
            gather(dst, lambda n: chip_at(2, pick(z_order, g, PA, n)), PA, first, HA, UA)
            for n in range(PA):
                part = pl.ds(n * HA, HA)
                dst[part, :] = dst[part, :] * sg_v[first : first + HA, :]
            a1[g, d] = send(dst, a1r.at[g, d], to)

    def a_two(g):
        for d, dx, first, to in ((0, 1, 0, xp), (1, -1, HA, xm)):
            dst = a2s.at[g, d]
            gather(dst, lambda n: chip_at(dx, pick(z_order, g, PA, n)), PA, 0, RA, UA)
            a1[g, d].wait_recv()
            for n in range(PA):
                with_part = pl.ds(n * RA + first, HA)
                alone = pl.ds(n * RA + HA - first, HA)
                dst[with_part, :] = dst[with_part, :] * sg_v[first : first + HA, :] + a1r[g, d, n * HA : (n + 1) * HA, :]
                dst[alone, :] = dst[alone, :] * sg_v[HA - first : RA - first, :]
            a2[g, d] = send(dst, a2r.at[g, d], to)

    def a_three(g):
        dst = a_sum.at[pl.ds(g * PA * RA, PA * RA)]
        gather(dst, lambda n: chip_at(0, pick(z_order, g, PA, n)), PA, 0, RA, UA)
        a2[g, 0].wait_recv()
        a2[g, 1].wait_recv()
        for n in range(PA):
            part = slice(n * RA, (n + 1) * RA)
            dst[part, :] = dst[part, :] * sg_v[0:RA, :] + (a2r[g, 0, part, :] + a2r[g, 1, part, :])

    def a_z(step):
        if step == 1:
            az[1, 0] = send(a_sum.at[pl.ds(0, HA)], azr.at[0, 0, pl.ds(0, HA)], zp)
            az[1, 1] = send(a_sum.at[pl.ds(HA, HA)], azr.at[1, 0, pl.ds(0, HA)], zm)
            return
        for d, to in ((0, zp), (1, zm)):
            at_row = (2 * step - 3 + d) * RA
            az[step - 1, d].wait_recv()
            if step == 2:
                part = pl.ds(at_row + d * HA, HA)
                a_sum[part, :] = a_sum[part, :] + azr[d, 0, 0:HA, :]
            else:
                part = pl.ds(at_row, RA)
                a_sum[part, :] = a_sum[part, :] + azr[d, step - 2]
            az[step, d] = send(a_sum.at[pl.ds(at_row, RA)], azr.at[d, step - 1], to)

    b1, b2, bx = {}, {}, {}

    def b_one(h):
        for d, first, to in ((0, RA, zp), (1, RA + HB, zm)):
            dst = b1s.at[h, d]
            gather(dst, lambda n: chip_at(pick(x_order, h, PB, n), 4), PB, first, HB, UB)
            for n in range(PB):
                part = pl.ds(n * HB, HB)
                dst[part, :] = dst[part, :] * sg_v[first : first + HB, :]
            b1[h, d] = send(dst, b1r.at[h, d], to)

    def b_next(h, step):
        for d, dz, to in ((0, 5 - step, zp), (1, step - 5, zm)):
            dst = b2s.at[h, d, step - 2]
            gather(dst, lambda n: chip_at(pick(x_order, h, PB, n), dz), PB, RA, RB, UB)
            if step == 2:
                b1[h, d].wait_recv()
                for n in range(PB):
                    first, rest = d * HB, HB - d * HB
                    with_part = pl.ds(n * RB + first, HB)
                    alone = pl.ds(n * RB + rest, HB)
                    dst[with_part, :] = (
                        dst[with_part, :] * sg_v[RA + first : RA + first + HB, :] + b1r[h, d, n * HB : (n + 1) * HB, :]
                    )
                    dst[alone, :] = dst[alone, :] * sg_v[RA + rest : RA + rest + HB, :]
            else:
                b2[h, d, step - 1].wait_recv()
                for n in range(PB):
                    part = slice(n * RB, (n + 1) * RB)
                    dst[part, :] = dst[part, :] * sg_v[RA:LIST, :] + b2r[h, d, step - 3, part, :]
            b2[h, d, step] = send(dst, b2r.at[h, d, step - 2], to)

    def b_five(h):
        dst = b_sum.at[pl.ds(h * PB * RB, PB * RB)]
        gather(dst, lambda n: chip_at(pick(x_order, h, PB, n), 0), PB, RA, RB, UB)
        b2[h, 0, 4].wait_recv()
        b2[h, 1, 4].wait_recv()
        for n in range(PB):
            part = slice(n * RB, (n + 1) * RB)
            dst[part, :] = dst[part, :] * sg_v[RA:LIST, :] + (b2r[h, 0, 2, part, :] + b2r[h, 1, 2, part, :])

    def b_x(step):
        if step == 1:
            bx[1, 0] = send(b_sum.at[pl.ds(0, HB)], bxr.at[0, 0, pl.ds(0, HB)], xp)
            bx[1, 1] = send(b_sum.at[pl.ds(HB, HB)], bxr.at[1, 0, pl.ds(0, HB)], xm)
            return
        for d, to in ((0, xp), (1, xm)):
            at_row = (1 + d) * RB
            bx[1, d].wait_recv()
            part = pl.ds(at_row + d * HB, HB)
            b_sum[part, :] = b_sum[part, :] + bxr[d, 0, 0:HB, :]
            bx[2, d] = send(b_sum.at[pl.ds(at_row, RB)], bxr.at[d, 1], to)

    scale = 1.0 / float(ROWS * CHIPS * 2) ** 0.5
    spread = {}

    def finish(first, rows, total):
        f_v[y, pl.ds(first, rows), :] = total * scale
        src = f_v.at[y, pl.ds(first, rows)]
        for o in range(1, NY):
            spread[first, o] = send(src, src, {"cols": lax.rem(y + o, NY)})
        spread[first, 0] = send(src, fp_v.at[pl.ds(first, rows)], partner)

    def a_finish():
        az[4, 0].wait_recv()
        az[4, 1].wait_recv()
        finish(0, RA, a_sum[7 * RA : 8 * RA, :] + (azr[0, 3] + azr[1, 3]))

    def b_finish():
        bx[2, 0].wait_recv()
        bx[2, 1].wait_recv()
        finish(RA, RB, b_sum[3 * RB : 4 * RB, :] + (bxr[0, 1] + bxr[1, 1]))

    with jax.named_scope("reduce early"):
        b_one(0)
        a_one(0)
        b_one(1)
        a_one(1)
        b_next(0, 2)
        a_two(0)
        a_one(2)
        b_next(1, 2)
    with jax.named_scope("reduce middle"):
        a_two(1)
        b_next(0, 3)
        a_one(3)
        a_three(0)
        a_z(1)
        b_next(1, 3)
        a_two(2)
        b_next(0, 4)
        a_three(1)
        a_z(2)
    with jax.named_scope("reduce late"):
        b_next(1, 4)
        a_two(3)
        a_three(2)
        a_z(3)
        b_five(0)
        b_x(1)
        b_five(1)
        b_x(2)
        a_three(3)
        a_z(4)
    with jax.named_scope("reduce end"):
        b_finish()
        a_finish()

    with jax.named_scope("spread over cols"):
        for first in (RA, 0):
            for o in range(1, NY):
                spread[first, o].wait_recv()
    with jax.named_scope("gram product"):
        mine_t = f_v[y].T
        for c in range(NY):
            whole = jnp.dot(mine_t, f_v[c], precision=lax.Precision.HIGHEST, preferred_element_type=F32)
            p_v[:, c * COLS : (c + 1) * COLS] = whole[:COLS, :COLS] + whole[COLS:, COLS:]

    def corner_copy(src_of, dst, n):
        copies = []
        for o in range(1, 8):
            to = lax.rem(corner + o, 8)
            copies.append(remote(src_of(to), dst, gs_sem.at[n], gr_sem.at[n], at(to // 2, z, lax.rem(to, 2))))
        return copies

    def rows_of(n):
        return pl.ds(pl.multiple_of(n * 8, 8), 8)

    def all_seven(ref, n, sems=gr_sem):
        seven = ref.at[pl.ds(0, 7)]
        pltpu.make_async_copy(seven, seven, sems.at[n]).wait()

    with jax.named_scope("gram rows"):
        first = corner_copy(lambda to: p_v.at[rows_of(to)], g1r.at[corner], 0)
        for copy in first:
            copy.start()
        g1r[corner] = p_v[rows_of(corner), :]
    with jax.named_scope("sketch out"):
        for part in (RA, 0):
            spread[part, 0].wait_recv()
        mine = f_v[y]
        other = fp_v[...]
        even = jnp.where(core == 0, mine, other).reshape(16, 8, 128)
        odd = jnp.where(core == 0, other, mine).reshape(16, 8, 128)
        upper = lax.broadcasted_iota(I32, (16, 8, 128), 1) < 4
        one = jnp.where(upper, even, pltpu.roll(odd, 4, 1))
        two = jnp.where(upper, pltpu.roll(even, 4, 1), odd)
        whole = jnp.stack([one, two], 1).reshape(256, 128).T
        sk_ref[...] = jnp.where(core == 0, whole[:COLS], whole[COLS:])
    with jax.named_scope("gram along z"):
        all_seven(g1r, 0)
        g2r[z] = jnp.sum(g1r[...], 0)
        second = []
        for o in range(1, NZ):
            to = at(x, z + o, core)
            second.append(remote(g2r.at[z], g2r.at[z], gs_sem.at[1], gr_sem.at[1], to))
            second[-1].start()
        all_seven(g2r, 1)
    with jax.named_scope("gram out"):
        g3r[corner] = jnp.sum(g2r[...], 0) * (1.0 / (LIST * 2 * CHIPS * 2))
        third = corner_copy(lambda to: g3r.at[corner], g3r.at[corner], 2)
        for copy in third:
            copy.start()
        all_seven(g3r, 2)
        g_ref[...] = g3r[...].reshape(COLS, NY * COLS)

    with jax.named_scope("drain"):
        ids_out.wait_send()
        sign_out.wait_send()

        def pair_done(q, _):
            pair_copy(q).wait_send()
            return 0

        lax.fori_loop(0, 8, pair_done, 0)

        pltpu.make_async_copy(ids_v.at[pl.ds(0, CHIPS - 1)], ids_v.at[pl.ds(0, CHIPS - 1)], is_sem).wait()
        for group in (a1, a2, az, b1, b2, bx, spread):
            for copy in group.values():
                copy.wait_send()
        for n in range(3):
            all_seven(g1r, n, gs_sem)


MESSAGES = 4 * GA + 8 + 8 * GB + 4 + 8


def on_device(matrix_t, signs, sample_ids):
    row = sample_ids & (ROWS - 1)
    index = ((row >> 7) & 1) * (ROWS // 2) + (row >> 8) * 128 + (row & 127)
    index = index.reshape(CHIPS, 2, KEEP).transpose(1, 0, 2).reshape(2, 1, LIST)
    vm = pltpu.VMEM
    dma = pltpu.SemaphoreType.DMA
    vmem_spec = pl.BlockSpec(memory_space=pltpu.VMEM)
    return pl.pallas_call(
        kernel,
        name="sketch_gram",
        out_shape=(
            jax.ShapeDtypeStruct((COLS, LIST * 2), F32),
            jax.ShapeDtypeStruct((COLS, NY * COLS), F32),
        ),
        in_specs=[pl.BlockSpec(memory_space=pl.ANY), vmem_spec, vmem_spec],
        out_specs=(vmem_spec, vmem_spec),
        scratch_shapes=[
            vm((8, COLS, 1024), F32),
            vm((8, COLS, 1024), F32),
            vm((64, 128), I32),
            vm((8, 4, 128, 128), F32),
            vm((ROWS, 128), F32),
            vm((1, LIST), I32),
            vm((CHIPS, 1, LIST), I32),
            pltpu.SMEM((CHIPS, 1, LIST), I32),
            vm((LIST, 128), F32),
            vm((GA, 2, PA * HA, 128), F32),
            vm((GA, 2, PA * HA, 128), F32),
            vm((GA, 2, PA * RA, 128), F32),
            vm((GA, 2, PA * RA, 128), F32),
            vm((NZ * RA, 128), F32),
            vm((2, 4, RA, 128), F32),
            vm((GB, 2, PB * HB, 128), F32),
            vm((GB, 2, PB * HB, 128), F32),
            vm((GB, 2, 3, PB * RB, 128), F32),
            vm((GB, 2, 3, PB * RB, 128), F32),
            vm((NX * RB, 128), F32),
            vm((2, 2, RB, 128), F32),
            vm((NY, LIST, 128), F32),
            vm((LIST, 128), F32),
            vm((COLS, NY * COLS), F32),
            vm((8, 8, NY * COLS), F32),
            vm((8, 8, NY * COLS), F32),
            vm((8, 8, NY * COLS), F32),
            dma((8,)),
            dma,
            dma((8,)),
            dma((8,)),
            dma((2,)),
            dma((2,)),
            dma,
            dma,
            dma((MESSAGES,)),
            dma((MESSAGES,)),
            dma((3,)),
            dma((3,)),
        ],
        compiler_params=pltpu.CompilerParams(
            collective_id=0, has_side_effects=True, vmem_limit_bytes=40 << 20
        ),
    )(matrix_t, signs.reshape(64, 128), index)


def solution(mesh):
    placed = (P("cols", "rows"), P("rows"), P("rows"))
    return jax.shard_map(
        on_device,
        mesh=mesh,
        in_specs=placed,
        out_specs=(P("cols", "rows"), P("cols", None)),
        check_vma=False,
    )
```

```python
import jax
import jax.numpy as jnp
from jax import lax
from jax.experimental import pallas as pl
from jax.experimental.pallas import tpu as pltpu
from jax.sharding import PartitionSpec as P

MESH = pl.DeviceIdType.MESH
F32, BF16, I32 = jnp.float32, jnp.bfloat16, jnp.int32

NX, NZ, NY = 4, 8, 4
CHIPS = NX * NZ
COLS, ROWS = 64, 8192
KEEP = 4
LIST = CHIPS * KEEP
RA = 64
HA = RA // 2
RB = LIST - RA
HB = RB // 2
Z_ORDER = (4, 3, -3, 2, -2, 1, -1, 0)
Z_GROUPS = ((0, 1), (1, 2), (3, 2), (5, 2), (7, 1))
X_FAR = (1, -1, 2)
X_ORDER = (2, 1, -1, 0)


def hadamard_rows(copies):
    shape = (128, 128 * copies)
    parity = lax.broadcasted_iota(I32, shape, 0) & lax.broadcasted_iota(I32, shape, 1) & 127
    for shift in (4, 2, 1):
        parity = parity ^ (parity >> shift)
    return (1 - 2 * (parity & 1)).astype(F32).astype(BF16)


def butterflies(parts):
    for stride in (1, 2, 4):
        done = list(parts)
        for i in range(8):
            if not i & stride:
                done[i] = parts[i] + parts[i | stride]
                done[i | stride] = parts[i] - parts[i | stride]
        parts = done
    return parts


def kernel(
    m_ref, s_ref, id_ref, out_ref,
    x_v, xp_v, s_v, sp_v, y_v, t_v, id_v, cls_v, idr_v, ids_v, ids_s, sg_v,
    a1s, a1r, a_sum, a4r, azr,
    b4s, b4r, bs, br, b_sum, bxr,
    f_v, fp_v, p_v, g1r, g2r, g3r,
    lx_sem, sm_sem, xs_sem, xr_sem, ps_sem, pr_sem, is_sem, ir_sem, rs_sem, rr_sem,
    gs_sem, gr_sem,
):
    me, y = lax.axis_index("rows"), lax.axis_index("cols")
    core, chip = me % 2, me // 2
    x, z = chip % NX, chip // NX
    corner = x * 2 + core

    def at(x_to, z_to, core_to):
        return {"rows": (lax.rem(z_to + NZ, NZ) * NX + lax.rem(x_to + NX, NX)) * 2 + core_to}

    partner = at(x, z, 1 - core)

    def remote(src, dst, send, recv, device):
        return pltpu.make_async_remote_copy(
            src_ref=src, dst_ref=dst, send_sem=send, recv_sem=recv, device_id=device, device_id_type=MESH
        )

    barrier = pltpu.get_barrier_semaphore()
    corners = []
    for o in range(1, 8):
        to = lax.rem(corner + o, 8)
        corners.append((to, at(to // 2, z, lax.rem(to, 2))))
    heights = [at(x, z + o, core) for o in range(1, NZ)]
    columns = [{"cols": lax.rem(y + o, NY)} for o in range(1, NY)]
    for device in [device for _, device in corners] + heights + columns:
        pl.semaphore_signal(barrier, inc=1, device_id=device, device_id_type=MESH)

    id_copy = pltpu.make_async_copy(id_ref, id_v, sm_sem.at[0])
    sign_copy = pltpu.make_async_copy(s_ref, s_v, sm_sem.at[1])
    id_copy.start()
    sign_copy.start()

    def own_copy(q):
        piece = pl.ds(pl.multiple_of(q * 1024, 1024), 1024)
        return pltpu.make_async_copy(m_ref.at[:, piece], x_v.at[q], lx_sem.at[q])

    for q in range(8):
        own_copy(q).start()

    id_copy.wait()
    row = id_v[...] & (ROWS - 1)
    place = ((row >> 7) & 1) * (ROWS // 2) + (row >> 8) * 128 + (row & 127)
    place = jnp.concatenate([place, jnp.zeros((6, 128), I32)], 0)
    lane = lax.broadcasted_iota(I32, (8, 128), 1)
    for c in range(2):
        packed = place if c == 0 else pltpu.roll(place, 128 - KEEP, 1)
        for i in range(4):
            packed = jnp.where((lane >> (2 + i)) & 1 == 1, pltpu.roll(packed, 128 - (KEEP << i), 1), packed)
        second = pltpu.roll(packed, 64, 1)
        cls_v[c] = jnp.where(lane[0:1] < 64, packed[0:1], second[1:2])

    pl.semaphore_wait(barrier, len(corners) + len(heights) + len(columns))

    sign_out = remote(s_ref, sp_v, ps_sem, pr_sem, partner)
    sign_out.start()

    def pair_copy(q):
        piece = pl.ds(pl.multiple_of(q * 1024, 1024), 1024)
        return remote(m_ref.at[:, piece], xp_v.at[q], xs_sem.at[q], xr_sem.at[q], partner)

    pair_copy(0).start()

    def wait_all(ref, slots, sem):
        piece = ref.at[pl.ds(0, slots)]
        pltpu.make_async_copy(piece, piece, sem).wait()

    for to, device in corners:
        remote(cls_v.at[lax.rem(to, 2)], idr_v.at[corner], is_sem.at[0], ir_sem.at[0], device).start()
    idr_v[corner] = cls_v[core]
    for q in range(1, 8):
        pair_copy(q).start()

    def lists_along_z():
        wait_all(idr_v, 7, ir_sem.at[0])
        for n in range(NX):
            ids_v[z * NX + n] = idr_v[2 * n] | ((idr_v[2 * n + 1] ^ (ROWS // 2)) << 16)
        four = ids_v.at[pl.ds(z * NX, NX)]
        for device in heights:
            remote(four, four, is_sem.at[1], ir_sem.at[1], device).start()

    block = lax.broadcasted_iota(I32, (LIST, 128), 0) // KEEP
    parity = block & chip
    for shift in (4, 2, 1):
        parity = parity ^ (parity >> shift)
    sg_v[...] = (1 - 2 * (parity & 1)).astype(F32)

    had = hadamard_rows(2)
    flip = (1 - 2 * core).astype(F32)
    sign_copy.wait()
    sign_out.wait_recv()

    with jax.named_scope("local transform"):

        def chunk(q, _):
            own_copy(q).wait()
            pair_copy(q).wait_recv()
            own_sign = s_v[pl.ds(pl.multiple_of(q * 8, 8), 8), :].astype(F32) * flip
            far_sign = sp_v[pl.ds(pl.multiple_of(q * 8, 8), 8), :].astype(F32)
            parts = []
            for i in range(8):
                lanes = slice(i * 128, (i + 1) * 128)
                parts.append(x_v[q, :, lanes] * own_sign[i : i + 1] + xp_v[q, :, lanes] * far_sign[i : i + 1])
            parts = butterflies(parts)
            for p in range(4):
                two = jnp.concatenate([parts[2 * p], parts[2 * p + 1]], 0)
                high = two.astype(BF16)
                low = (two - high.astype(F32)).astype(BF16)
                y_v[q, p] = lax.dot_general(
                    had, jnp.concatenate([high, low], 1), (((1,), (1,)), ((), ())), preferred_element_type=F32
                )
            return 0

        lax.fori_loop(0, 4, chunk, 0)
        lists_along_z()
        lax.fori_loop(4, 8, chunk, 0)

    with jax.named_scope("across chunks"):

        def across(i, _):
            p = i // 4
            for t in range(4):
                row = pl.multiple_of((i % 4) * 32 + t * 8, 8)
                parts = butterflies([y_v[q, p, pl.ds(row, 8), :] for q in range(8)])
                for q in range(8):
                    to = pl.multiple_of(q * 512 + p * 128 + row, 8)
                    t_v[pl.ds(to, 8), :] = parts[q]
                    t_v[pl.ds(to + ROWS // 2, 8), :] = pltpu.roll(parts[q], 64, 1)
            return 0

        lax.fori_loop(0, 16, across, 0)
    wait_all(ids_v, 7 * NX, ir_sem.at[1])
    lists = pltpu.make_async_copy(ids_v, ids_s, sm_sem.at[2])
    lists.start()
    lists.wait()

    half = lax.broadcasted_iota(I32, (1, 128), 1) < 64

    def gather(dst, at_row, of, first, rows):
        for start in range(first, first + rows, 32):
            got = []
            for j in range(start, start + 32):
                if j % KEEP == 0:
                    sign = sg_v[j : j + 1, :]
                word = ids_s[of, 0, j]
                a = t_v[pl.ds(word & 0xFFFF, 1), :]
                b = t_v[pl.ds(word >> 16, 1), :]
                got.append(jnp.where(half, a, b) * sign)
            for u in range(32):
                dst[pl.ds(at_row + (start - first + u), 1), :] = got[u]

    count = [0]

    def send(src, dst, device):
        n = count[0]
        count[0] += 1
        copy = remote(src, dst, rs_sem.at[n], rr_sem.at[n], device)
        copy.start()
        return copy

    ups = (at(x, z + 1, core), at(x, z - 1, core))
    twos = (at(x, z + 2, core), at(x, z - 2, core))

    def chip_at(dx, dz):
        return lax.rem(z + dz + NZ, NZ) * NX + lax.rem(x + dx + NX, NX)

    def pick(values, n):
        value = jnp.int32(values[0])
        for k in range(1, len(values)):
            value = jnp.where(n == k, values[k], value)
        return value

    a1, az = {}, {}

    def a_send(g):
        place, width = Z_GROUPS[g]

        def one(n, _):
            slot = n // width
            dz = pick(Z_ORDER[place : place + width], n - slot * width)
            at_row = pl.multiple_of((slot * (NZ - width) + place + n) * RA, RA)
            gather(a1s, at_row, chip_at(pick(X_FAR, slot), dz), 0, RA)
            return 0

        lax.fori_loop(0, 3 * width, one, 0)
        for slot in range(3):
            part = pl.ds((slot * NZ + place) * RA, width * RA)
            a1[g, slot] = send(a1s.at[part], a1r.at[part], at(x + X_FAR[slot], z, core))

    def a_own(g):
        place, width = Z_GROUPS[g]

        def one(n, _):
            at_row = pl.multiple_of((place + n) * RA, RA)
            gather(a_sum, at_row, chip_at(0, pick(Z_ORDER[place : place + width], n)), 0, RA)
            return 0

        lax.fori_loop(0, width, one, 0)

    def a_add(g):
        place, width = Z_GROUPS[g]
        total = a_sum[place * RA : (place + width) * RA, :]
        for slot in range(3):
            a1[g, slot].wait_recv()
            total = total + a1r[(slot * NZ + place) * RA : (slot * NZ + place + width) * RA, :]
        a_sum[place * RA : (place + width) * RA, :] = total

    def a_z(step):
        for d in range(2):
            if step == 4:
                az[4, d] = send(a_sum.at[pl.ds(d * HA, HA)], a4r.at[d], twos[d])
                continue
            at_row = (7 - 2 * step + d) * RA
            if step == 2:
                az[4, d].wait_recv()
                part = pl.ds(at_row + d * HA, HA)
                a_sum[part, :] = a_sum[part, :] + a4r[d]
            if step < 3:
                az[step + 1, d].wait_recv()
                part = pl.ds(at_row, RA)
                a_sum[part, :] = a_sum[part, :] + azr[step, d]
            az[step, d] = send(a_sum.at[pl.ds(at_row, RA)], azr.at[step - 1, d], ups[d])

    b4, bz, bx = {}, {}, {}

    def b_far():
        def one(h, _):
            gather(b4s, pl.multiple_of(h * RB, RB), chip_at(pick(X_ORDER, h), 4), RA, RB)
            return 0

        lax.fori_loop(0, NX, one, 0)
        for h in range(NX):
            for d in range(2):
                b4[h, d] = send(b4s.at[pl.ds(h * RB + d * HB, HB)], b4r.at[h, d], twos[d])

    def b_own(step, first, last):
        def one(n, _):
            d = lax.rem(n, 2)
            h = n // 2
            dst = bs.at[step - 1, h, d]
            gather(dst, 0, chip_at(pick(X_ORDER, h), step - 2 * step * d), RA, RB)
            return 0

        lax.fori_loop(2 * first, 2 * last, one, 0)

    def b_z(step, h):
        for d in range(2):
            src = bs.at[step - 1, h, d]
            if step == 2:
                b4[h, d].wait_recv()
                part = pl.ds(d * HB, HB)
                src[part, :] = src[part, :] + b4r[h, d]
            if step < 3:
                bz[step + 1, h, d].wait_recv()
                src[...] = src[...] + br[step, h, d]
            bz[step, h, d] = send(src, br.at[step - 1, h, d], ups[d])

    def b_home():
        def one(h, _):
            gather(b_sum, pl.multiple_of(h * RB, RB), chip_at(pick(X_ORDER, h), 0), RA, RB)
            return 0

        lax.fori_loop(0, NX, one, 0)

    def b_x(h):
        part = pl.ds(h * RB, RB)
        bz[1, h, 0].wait_recv()
        bz[1, h, 1].wait_recv()
        b_sum[part, :] = b_sum[part, :] + (br[0, h, 0] + br[0, h, 1])
        if X_ORDER[h]:
            bx[h] = send(b_sum.at[part], bxr.at[h], at(x + X_ORDER[h], z, core))

    scale = 1.0 / float(ROWS * CHIPS * 2) ** 0.5
    spread = {}

    def finish(first, rows, total):
        f_v[y, pl.ds(first, rows), :] = total * scale
        src = f_v.at[y, pl.ds(first, rows)]
        for o in range(1, NY):
            spread[first, o] = send(src, src, columns[o - 1])
        spread[first, 0] = send(src, fp_v.at[pl.ds(first, rows)], partner)

    def a_finish():
        az[1, 0].wait_recv()
        az[1, 1].wait_recv()
        finish(0, RA, a_sum[7 * RA : 8 * RA, :] + (azr[0, 0] + azr[0, 1]))

    def b_finish():
        total = b_sum[3 * RB : 4 * RB, :]
        for h in range(3):
            bx[h].wait_recv()
            total = total + bxr[h]
        finish(RA, RB, total)

    with jax.named_scope("reduce early"):
        b_far()
        a_send(0)
        b_own(3, 0, 2)
        b_z(3, 0)
        b_z(3, 1)
        b_own(3, 2, 4)
        b_z(3, 2)
        b_z(3, 3)
        a_send(1)
        b_own(2, 0, 4)
        a_own(0)
        a_send(2)
    with jax.named_scope("reduce middle"):
        b_z(2, 0)
        b_z(2, 1)
        a_add(0)
        a_z(4)
        b_z(2, 2)
        b_z(2, 3)
        a_send(3)
        b_own(1, 0, 4)
        a_own(1)
        a_add(1)
        a_z(3)
        a_send(4)
        a_own(2)
        b_z(1, 0)
        b_z(1, 1)
        b_z(1, 2)
        b_z(1, 3)
    with jax.named_scope("reduce late"):
        b_home()
        a_own(3)
        a_own(4)
        a_add(2)
        a_z(2)
        b_x(0)
        b_x(1)
        b_x(2)
        b_x(3)
        a_add(3)
        a_z(1)
        a_add(4)
    with jax.named_scope("reduce end"):
        b_finish()
        a_finish()

    with jax.named_scope("spread over cols"):
        for first in (RA, 0):
            for o in range(1, NY):
                spread[first, o].wait_recv()
    with jax.named_scope("gram product"):
        mine_t = f_v[y].T
        for c in range(NY):
            whole = jnp.dot(mine_t, f_v[c], precision=lax.Precision.HIGHEST, preferred_element_type=F32)
            p_v[:, c * COLS : (c + 1) * COLS] = whole[:COLS, :COLS] + whole[COLS:, COLS:]

    def corner_copy(src_of, dst, n):
        return [remote(src_of(to), dst, gs_sem.at[n], gr_sem.at[n], device) for to, device in corners]

    def rows_of(n):
        return pl.ds(pl.multiple_of(n * 8, 8), 8)

    def all_seven(ref, n, sems=gr_sem):
        seven = ref.at[pl.ds(0, 7)]
        pltpu.make_async_copy(seven, seven, sems.at[n]).wait()

    with jax.named_scope("gram rows"):
        first = corner_copy(lambda to: p_v.at[rows_of(to)], g1r.at[corner], 0)
        for copy in first:
            copy.start()
        g1r[corner] = p_v[rows_of(corner), :]
    with jax.named_scope("drain"):
        sign_out.wait_send()

        def pair_done(q, _):
            pair_copy(q).wait_send()
            return 0

        lax.fori_loop(0, 8, pair_done, 0)

        wait_all(idr_v, 7, is_sem.at[0])
        wait_all(ids_v, 7 * NX, is_sem.at[1])
        for group in (a1, az, b4, bz, bx):
            for copy in group.values():
                copy.wait_send()
    with jax.named_scope("sketch out"):
        for part in (RA, 0):
            spread[part, 0].wait_recv()
        mine = f_v[y]
        other = fp_v[...]
        even = jnp.where(core == 0, mine, other).reshape(16, 8, 128)
        odd = jnp.where(core == 0, other, mine).reshape(16, 8, 128)
        upper = lax.broadcasted_iota(I32, (16, 8, 128), 1) < 4
        one = jnp.where(upper, even, pltpu.roll(odd, 4, 1))
        two = jnp.where(upper, pltpu.roll(even, 4, 1), odd)
        whole = jnp.stack([one, two], 1).reshape(256, 128).T
        out_ref[:COLS, :] = jnp.where(core == 0, whole[:COLS], whole[COLS:])
    with jax.named_scope("gram along z"):
        all_seven(g1r, 0)
        g2r[z] = jnp.sum(g1r[...], 0)
        second = []
        for device in heights:
            second.append(remote(g2r.at[z], g2r.at[z], gs_sem.at[1], gr_sem.at[1], device))
            second[-1].start()
        all_seven(g2r, 1)
    with jax.named_scope("gram out"):
        g3r[corner] = jnp.sum(g2r[...], 0)
        third = corner_copy(lambda to: g3r.at[corner], g3r.at[corner], 2)
        for copy in third:
            copy.start()
        all_seven(g3r, 2)
        out_ref[COLS:, :] = g3r[...].reshape(COLS, NY * COLS)

    for copy in spread.values():
        copy.wait_send()
    for n in range(3):
        all_seven(g1r, n, gs_sem)


MESSAGES = 15 + 8 + 8 + 24 + 3 + 8


def on_device(matrix_t, signs, sample_ids):
    vm = pltpu.VMEM
    dma = pltpu.SemaphoreType.DMA
    vmem_spec = pl.BlockSpec(memory_space=pltpu.VMEM)
    operands = matrix_t, signs.reshape(64, 128), sample_ids.reshape(2, 128)
    both = pl.pallas_call(
        kernel,
        name="sketch_gram",
        out_shape=jax.ShapeDtypeStruct((2 * COLS, NY * COLS), F32),
        in_specs=[pl.BlockSpec(memory_space=pl.ANY)] * 3,
        out_specs=vmem_spec,
        scratch_shapes=[
            vm((8, COLS, 1024), F32),
            vm((8, COLS, 1024), F32),
            vm((64, 128), I32),
            vm((64, 128), I32),
            vm((8, 4, 128, 128), F32),
            vm((ROWS, 128), F32),
            vm((2, 128), I32),
            vm((2, 1, LIST), I32),
            vm((8, 1, LIST), I32),
            vm((CHIPS, 1, LIST), I32),
            pltpu.SMEM((CHIPS, 1, LIST), I32),
            vm((LIST, 128), F32),
            vm((3 * NZ * RA, 128), F32),
            vm((3 * NZ * RA, 128), F32),
            vm((NZ * RA, 128), F32),
            vm((2, HA, 128), F32),
            vm((3, 2, RA, 128), F32),
            vm((NX * RB, 128), F32),
            vm((NX, 2, HB, 128), F32),
            vm((3, NX, 2, RB, 128), F32),
            vm((3, NX, 2, RB, 128), F32),
            vm((NX * RB, 128), F32),
            vm((3, RB, 128), F32),
            vm((NY, LIST, 128), F32),
            vm((LIST, 128), F32),
            vm((COLS, NY * COLS), F32),
            vm((8, 8, NY * COLS), F32),
            vm((8, 8, NY * COLS), F32),
            vm((8, 8, NY * COLS), F32),
            dma((8,)),
            dma((3,)),
            dma((8,)),
            dma((8,)),
            dma,
            dma,
            dma((2,)),
            dma((2,)),
            dma((MESSAGES,)),
            dma((MESSAGES,)),
            dma((3,)),
            dma((3,)),
        ],
        compiler_params=pltpu.CompilerParams(
            collective_id=0, has_side_effects=True, vmem_limit_bytes=40 << 20
        ),
    )(*(pltpu.with_memory_space_constraint(v, pltpu.HBM) for v in operands))
    return both[:COLS], both[COLS:] * (1.0 / (LIST * 2 * CHIPS * 2))


def solution(mesh):
    placed = (P("cols", "rows"), P("rows"), P("rows"))
    return jax.shard_map(
        on_device,
        mesh=mesh,
        in_specs=placed,
        out_specs=(P("cols", "rows"), P("cols", None)),
        check_vma=False,
    )
```

```python
import jax
import jax.numpy as jnp
from jax import lax
from jax.experimental import pallas as pl
from jax.experimental.pallas import tpu as pltpu
from jax.sharding import PartitionSpec as P

MESH = pl.DeviceIdType.MESH
F32, BF16, I32 = jnp.float32, jnp.bfloat16, jnp.int32

NX, NZ, NY = 4, 8, 4
CHIPS = NX * NZ
COLS, ROWS = 64, 8192
KEEP = 4
LIST = CHIPS * KEEP
RA = 80
HA = RA // 2
RB = LIST - RA
HB = RB // 2
Z_ORDER = (4, 3, -3, 2, -2, 1, -1, 0)
Z_GROUPS = ((0, 1), (1, 2), (3, 2), (5, 2), (7, 1))
F_GROUPS = ((0, 3), (3, 5))
UNROLL = {RA: 40, HA: 40, RB: 48}
X_ORDER = (2, 1, -1, 0)


def hadamard_rows(copies):
    shape = (128, 128 * copies)
    parity = lax.broadcasted_iota(I32, shape, 0) & lax.broadcasted_iota(I32, shape, 1) & 127
    for shift in (4, 2, 1):
        parity = parity ^ (parity >> shift)
    return (1 - 2 * (parity & 1)).astype(F32).astype(BF16)


def butterflies(parts):
    for stride in (1, 2, 4):
        done = list(parts)
        for i in range(8):
            if not i & stride:
                done[i] = parts[i] + parts[i | stride]
                done[i | stride] = parts[i] - parts[i | stride]
        parts = done
    return parts


def kernel(
    m_ref, s_ref, id_ref, out_ref,
    x_v, xp_v, s_v, sp_v, y_v, t_v, id_v, cls_v, idr_v, ids_v, ids_s, sg_v,
    afs, afr, ans, anr, a_sum, a4r, azr,
    b4s, b4r, bs, br, b_sum, bxr,
    f_v, fp_v, p_v, g1r, g2r, g3r,
    lx_sem, sm_sem, xs_sem, xr_sem, ps_sem, pr_sem, is_sem, ir_sem, rs_sem, rr_sem,
    gs_sem, gr_sem,
):
    me, y = lax.axis_index("rows"), lax.axis_index("cols")
    core, chip = me % 2, me // 2
    x, z = chip % NX, chip // NX
    corner = x * 2 + core

    def at(x_to, z_to, core_to):
        return {"rows": (lax.rem(z_to + NZ, NZ) * NX + lax.rem(x_to + NX, NX)) * 2 + core_to}

    partner = at(x, z, 1 - core)

    def remote(src, dst, send, recv, device):
        return pltpu.make_async_remote_copy(
            src_ref=src, dst_ref=dst, send_sem=send, recv_sem=recv, device_id=device, device_id_type=MESH
        )

    barrier = pltpu.get_barrier_semaphore()
    corners = []
    for o in range(1, 8):
        to = lax.rem(corner + o, 8)
        corners.append((to, at(to // 2, z, lax.rem(to, 2))))
    heights = [at(x, z + o, core) for o in range(1, NZ)]
    columns = [{"cols": lax.rem(y + o, NY)} for o in range(1, NY)]
    for device in [device for _, device in corners] + heights + columns:
        pl.semaphore_signal(barrier, inc=1, device_id=device, device_id_type=MESH)

    id_copy = pltpu.make_async_copy(id_ref, id_v, sm_sem.at[0])
    sign_copy = pltpu.make_async_copy(s_ref, s_v, sm_sem.at[1])
    id_copy.start()
    sign_copy.start()

    def own_copy(q):
        piece = pl.ds(pl.multiple_of(q * 1024, 1024), 1024)
        return pltpu.make_async_copy(m_ref.at[:, piece], x_v.at[q], lx_sem.at[q])

    for q in range(8):
        own_copy(q).start()

    id_copy.wait()
    row = id_v[...] & (ROWS - 1)
    place = ((row >> 7) & 1) * (ROWS // 2) + (row >> 8) * 128 + (row & 127)
    place = jnp.concatenate([place, jnp.zeros((6, 128), I32)], 0)
    lane = lax.broadcasted_iota(I32, (8, 128), 1)
    for c in range(2):
        packed = place if c == 0 else pltpu.roll(place, 128 - KEEP, 1)
        for i in range(4):
            packed = jnp.where((lane >> (2 + i)) & 1 == 1, pltpu.roll(packed, 128 - (KEEP << i), 1), packed)
        second = pltpu.roll(packed, 64, 1)
        cls_v[c] = jnp.where(lane[0:1] < 64, packed[0:1], second[1:2])

    pl.semaphore_wait(barrier, len(corners) + len(heights) + len(columns))

    sign_out = remote(s_ref, sp_v, ps_sem, pr_sem, partner)
    sign_out.start()

    def pair_copy(q):
        piece = pl.ds(pl.multiple_of(q * 1024, 1024), 1024)
        return remote(m_ref.at[:, piece], xp_v.at[q], xs_sem.at[q], xr_sem.at[q], partner)

    pair_copy(0).start()

    def wait_all(ref, slots, sem):
        piece = ref.at[pl.ds(0, slots)]
        pltpu.make_async_copy(piece, piece, sem).wait()

    for to, device in corners:
        remote(cls_v.at[lax.rem(to, 2)], idr_v.at[corner], is_sem.at[0], ir_sem.at[0], device).start()
    idr_v[corner] = cls_v[core]
    for q in range(1, 8):
        pair_copy(q).start()

    def lists_along_z():
        wait_all(idr_v, 7, ir_sem.at[0])
        for n in range(NX):
            ids_v[z * NX + n] = idr_v[2 * n] | ((idr_v[2 * n + 1] ^ (ROWS // 2)) << 16)
        four = ids_v.at[pl.ds(z * NX, NX)]
        for device in heights:
            remote(four, four, is_sem.at[1], ir_sem.at[1], device).start()

    block = lax.broadcasted_iota(I32, (LIST, 128), 0) // KEEP
    parity = block & chip
    for shift in (4, 2, 1):
        parity = parity ^ (parity >> shift)
    sg_v[...] = (1 - 2 * (parity & 1)).astype(F32)

    had = hadamard_rows(2)
    flip = (1 - 2 * core).astype(F32)
    sign_copy.wait()
    sign_out.wait_recv()

    with jax.named_scope("local transform"):

        def chunk(q, _):
            own_copy(q).wait()
            pair_copy(q).wait_recv()
            own_sign = s_v[pl.ds(pl.multiple_of(q * 8, 8), 8), :].astype(F32) * flip
            far_sign = sp_v[pl.ds(pl.multiple_of(q * 8, 8), 8), :].astype(F32)
            parts = []
            for i in range(8):
                lanes = slice(i * 128, (i + 1) * 128)
                parts.append(x_v[q, :, lanes] * own_sign[i : i + 1] + xp_v[q, :, lanes] * far_sign[i : i + 1])
            parts = butterflies(parts)
            for p in range(4):
                two = jnp.concatenate([parts[2 * p], parts[2 * p + 1]], 0)
                high = two.astype(BF16)
                low = (two - high.astype(F32)).astype(BF16)
                y_v[q, p] = lax.dot_general(
                    had, jnp.concatenate([high, low], 1), (((1,), (1,)), ((), ())), preferred_element_type=F32
                )
            return 0

        lax.fori_loop(0, 4, chunk, 0)
        lists_along_z()
        lax.fori_loop(4, 8, chunk, 0)

    with jax.named_scope("across chunks"):

        def across(i, _):
            p = i // 4
            for t in range(4):
                row = pl.multiple_of((i % 4) * 32 + t * 8, 8)
                parts = butterflies([y_v[q, p, pl.ds(row, 8), :] for q in range(8)])
                for q in range(8):
                    to = pl.multiple_of(q * 512 + p * 128 + row, 8)
                    t_v[pl.ds(to, 8), :] = parts[q]
                    t_v[pl.ds(to + ROWS // 2, 8), :] = pltpu.roll(parts[q], 64, 1)
            return 0

        lax.fori_loop(0, 16, across, 0)
    wait_all(ids_v, 7 * NX, ir_sem.at[1])
    lists = pltpu.make_async_copy(ids_v, ids_s, sm_sem.at[2])
    lists.start()
    lists.wait()

    half = lax.broadcasted_iota(I32, (1, 128), 1) < 64

    def gather(dst, at_row, of, first, rows):
        unroll = UNROLL[rows]
        for start in range(first, first + rows, unroll):
            got = []
            for j in range(start, start + unroll):
                if j == start or j % KEEP == 0:
                    sign = sg_v[j : j + 1, :]
                word = ids_s[of, 0, j]
                a = t_v[pl.ds(word & 0xFFFF, 1), :]
                b = t_v[pl.ds(word >> 16, 1), :]
                got.append(jnp.where(half, a, b) * sign)
            for u in range(unroll):
                dst[pl.ds(at_row + (start - first + u), 1), :] = got[u]

    count = [0]

    def send(src, dst, device):
        n = count[0]
        count[0] += 1
        copy = remote(src, dst, rs_sem.at[n], rr_sem.at[n], device)
        copy.start()
        return copy

    ups = (at(x, z + 1, core), at(x, z - 1, core))
    twos = (at(x, z + 2, core), at(x, z - 2, core))

    def chip_at(dx, dz):
        return lax.rem(z + dz + NZ, NZ) * NX + lax.rem(x + dx + NX, NX)

    def pick(values, n):
        value = jnp.int32(values[0])
        for k in range(1, len(values)):
            value = jnp.where(n == k, values[k], value)
        return value

    sides = (at(x + 1, z, core), at(x - 1, z, core))
    af, an, az = {}, {}, {}

    def a_far(g):
        place, width = F_GROUPS[g]

        def one(n, _):
            chip_to = chip_at(2, pick(Z_ORDER[place : place + width], n))
            at_row = pl.multiple_of((place + n) * HA, HA)
            gather(afs.at[0], at_row, chip_to, 0, HA)
            gather(afs.at[1], at_row, chip_to, HA, HA)
            return 0

        lax.fori_loop(0, width, one, 0)
        part = pl.ds(place * HA, width * HA)
        for d in range(2):
            af[g, d] = send(afs.at[d, part], afr.at[d, part], sides[d])

    def a_near(place, last):
        def one(n, _):
            d = lax.rem(n, 2)
            k = n // 2
            at_row = pl.multiple_of(k * RA, RA)
            gather(ans.at[d], at_row, chip_at(1 - 2 * d, pick(Z_ORDER, k)), 0, RA)
            return 0

        lax.fori_loop(2 * place, 2 * last, one, 0)

    def a_x(g):
        place, width = Z_GROUPS[g]
        part = pl.ds(place * RA, width * RA)
        for d in range(2):
            for f in range(2):
                if F_GROUPS[f][0] == place:
                    af[f, d].wait_recv()
            for k in range(place, place + width):
                rows = pl.ds(k * RA + d * HA, HA)
                ans[d, rows, :] = ans[d, rows, :] + afr[d, k * HA : (k + 1) * HA, :]
            an[g, d] = send(ans.at[d, part], anr.at[d, part], sides[d])

    def a_own():
        def one(n, _):
            gather(a_sum, pl.multiple_of(n * RA, RA), chip_at(0, pick(Z_ORDER, n)), 0, RA)
            return 0

        lax.fori_loop(0, NZ, one, 0)

    def a_add(g):
        place, width = Z_GROUPS[g]
        an[g, 0].wait_recv()
        an[g, 1].wait_recv()
        part = slice(place * RA, (place + width) * RA)
        a_sum[part, :] = a_sum[part, :] + (anr[0, part, :] + anr[1, part, :])

    def a_z(step):
        for d in range(2):
            if step == 4:
                az[4, d] = send(a_sum.at[pl.ds(d * HA, HA)], a4r.at[d], twos[d])
                continue
            at_row = (7 - 2 * step + d) * RA
            if step == 2:
                az[4, d].wait_recv()
                part = pl.ds(at_row + d * HA, HA)
                a_sum[part, :] = a_sum[part, :] + a4r[d]
                az[3, d].wait_recv()
                part = pl.ds(at_row, RA)
                a_sum[part, :] = a_sum[part, :] + azr[2, d]
            to = twos[d] if step == 2 else ups[d]
            az[step, d] = send(a_sum.at[pl.ds(at_row, RA)], azr.at[step - 1, d], to)

    b4, bz, bx = {}, {}, {}

    def b_far():
        def one(h, _):
            gather(b4s, pl.multiple_of(h * RB, RB), chip_at(pick(X_ORDER, h), 4), RA, RB)
            return 0

        lax.fori_loop(0, NX, one, 0)
        for h in range(NX):
            for d in range(2):
                b4[h, d] = send(b4s.at[pl.ds(h * RB + d * HB, HB)], b4r.at[h, d], twos[d])

    def b_own(step, first, last):
        def one(n, _):
            d = lax.rem(n, 2)
            h = n // 2
            dst = bs.at[step - 1, h, d]
            gather(dst, 0, chip_at(pick(X_ORDER, h), step - 2 * step * d), RA, RB)
            return 0

        lax.fori_loop(2 * first, 2 * last, one, 0)

    def b_z(step, h):
        for d in range(2):
            src = bs.at[step - 1, h, d]
            if step == 2:
                b4[h, d].wait_recv()
                part = pl.ds(d * HB, HB)
                src[part, :] = src[part, :] + b4r[h, d]
            if step < 3:
                bz[step + 1, h, d].wait_recv()
                src[...] = src[...] + br[step, h, d]
            bz[step, h, d] = send(src, br.at[step - 1, h, d], ups[d])

    def b_home():
        def one(h, _):
            gather(b_sum, pl.multiple_of(h * RB, RB), chip_at(pick(X_ORDER, h), 0), RA, RB)
            return 0

        lax.fori_loop(0, NX, one, 0)

    def b_x(h):
        part = pl.ds(h * RB, RB)
        bz[1, h, 0].wait_recv()
        bz[1, h, 1].wait_recv()
        b_sum[part, :] = b_sum[part, :] + (br[0, h, 0] + br[0, h, 1])
        if X_ORDER[h]:
            bx[h] = send(b_sum.at[part], bxr.at[h], at(x + X_ORDER[h], z, core))

    scale = 1.0 / float(ROWS * CHIPS * 2) ** 0.5
    spread = {}

    def finish(first, rows, total):
        f_v[y, pl.ds(first, rows), :] = total * scale
        src = f_v.at[y, pl.ds(first, rows)]
        for o in range(1, NY):
            spread[first, o] = send(src, src, columns[o - 1])
        spread[first, 0] = send(src, fp_v.at[pl.ds(first, rows)], partner)

    def a_finish():
        total = a_sum[7 * RA : 8 * RA, :]
        for step in (1, 2):
            az[step, 0].wait_recv()
            az[step, 1].wait_recv()
            total = total + (azr[step - 1, 0] + azr[step - 1, 1])
        finish(0, RA, total)

    def b_finish():
        total = b_sum[3 * RB : 4 * RB, :]
        for h in range(3):
            bx[h].wait_recv()
            total = total + bxr[h]
        finish(RA, RB, total)

    with jax.named_scope("reduce early"):
        b_far()
        a_far(0)
        b_own(3, 0, 2)
        b_z(3, 0)
        b_z(3, 1)
        a_far(1)
        b_own(3, 2, 4)
        b_z(3, 2)
        b_z(3, 3)
        a_near(0, 3)
        b_own(2, 0, 4)
    with jax.named_scope("reduce middle"):
        a_x(0)
        a_x(1)
        b_z(2, 0)
        b_z(2, 1)
        b_z(2, 2)
        b_z(2, 3)
        a_near(3, 8)
        a_x(2)
        a_x(3)
        a_x(4)
        b_own(1, 0, 4)
        a_own()
    with jax.named_scope("reduce late"):
        a_add(0)
        a_z(4)
        b_z(1, 0)
        b_z(1, 1)
        a_add(1)
        a_z(3)
        b_z(1, 2)
        b_z(1, 3)
        b_home()
        a_add(2)
        a_z(2)
        b_x(0)
        b_x(1)
        a_add(3)
        a_z(1)
        b_x(2)
        b_x(3)
        a_add(4)
    with jax.named_scope("reduce end"):
        b_finish()
        a_finish()

    with jax.named_scope("spread over cols"):
        for first in (RA, 0):
            for o in range(1, NY):
                spread[first, o].wait_recv()
    with jax.named_scope("gram product"):
        mine_t = f_v[y].T
        for c in range(NY):
            whole = jnp.dot(mine_t, f_v[c], precision=lax.Precision.HIGHEST, preferred_element_type=F32)
            p_v[:, c * COLS : (c + 1) * COLS] = whole[:COLS, :COLS] + whole[COLS:, COLS:]

    def corner_copy(src_of, dst, n):
        return [remote(src_of(to), dst, gs_sem.at[n], gr_sem.at[n], device) for to, device in corners]

    def rows_of(n):
        return pl.ds(pl.multiple_of(n * 8, 8), 8)

    def all_seven(ref, n, sems=gr_sem):
        seven = ref.at[pl.ds(0, 7)]
        pltpu.make_async_copy(seven, seven, sems.at[n]).wait()

    with jax.named_scope("gram rows"):
        first = corner_copy(lambda to: p_v.at[rows_of(to)], g1r.at[corner], 0)
        for copy in first:
            copy.start()
        g1r[corner] = p_v[rows_of(corner), :]
    with jax.named_scope("drain"):
        sign_out.wait_send()

        def pair_done(q, _):
            pair_copy(q).wait_send()
            return 0

        lax.fori_loop(0, 8, pair_done, 0)

        wait_all(idr_v, 7, is_sem.at[0])
        wait_all(ids_v, 7 * NX, is_sem.at[1])
        for group in (af, an, az, b4, bz, bx):
            for copy in group.values():
                copy.wait_send()
    with jax.named_scope("sketch out"):
        for part in (RA, 0):
            spread[part, 0].wait_recv()
        mine = f_v[y]
        other = fp_v[...]
        even = jnp.where(core == 0, mine, other).reshape(16, 8, 128)
        odd = jnp.where(core == 0, other, mine).reshape(16, 8, 128)
        upper = lax.broadcasted_iota(I32, (16, 8, 128), 1) < 4
        one = jnp.where(upper, even, pltpu.roll(odd, 4, 1))
        two = jnp.where(upper, pltpu.roll(even, 4, 1), odd)
        whole = jnp.stack([one, two], 1).reshape(256, 128).T
        out_ref[:COLS, :] = jnp.where(core == 0, whole[:COLS], whole[COLS:])
    with jax.named_scope("gram along z"):
        all_seven(g1r, 0)
        g2r[z] = jnp.sum(g1r[...], 0)
        second = []
        for device in heights:
            second.append(remote(g2r.at[z], g2r.at[z], gs_sem.at[1], gr_sem.at[1], device))
            second[-1].start()
        all_seven(g2r, 1)
    with jax.named_scope("gram out"):
        g3r[corner] = jnp.sum(g2r[...], 0)
        third = corner_copy(lambda to: g3r.at[corner], g3r.at[corner], 2)
        for copy in third:
            copy.start()
        all_seven(g3r, 2)
        out_ref[COLS:, :] = g3r[...].reshape(COLS, NY * COLS)

    for copy in spread.values():
        copy.wait_send()
    for n in range(3):
        all_seven(g1r, n, gs_sem)


MESSAGES = 4 + 10 + 8 + 8 + 24 + 3 + 8


def on_device(matrix_t, signs, sample_ids):
    vm = pltpu.VMEM
    dma = pltpu.SemaphoreType.DMA
    vmem_spec = pl.BlockSpec(memory_space=pltpu.VMEM)
    operands = matrix_t, signs.reshape(64, 128), sample_ids.reshape(2, 128)
    both = pl.pallas_call(
        kernel,
        name="sketch_gram",
        out_shape=jax.ShapeDtypeStruct((2 * COLS, NY * COLS), F32),
        in_specs=[pl.BlockSpec(memory_space=pl.ANY)] * 3,
        out_specs=vmem_spec,
        scratch_shapes=[
            vm((8, COLS, 1024), F32),
            vm((8, COLS, 1024), F32),
            vm((64, 128), I32),
            vm((64, 128), I32),
            vm((8, 4, 128, 128), F32),
            vm((ROWS, 128), F32),
            vm((2, 128), I32),
            vm((2, 1, LIST), I32),
            vm((8, 1, LIST), I32),
            vm((CHIPS, 1, LIST), I32),
            pltpu.SMEM((CHIPS, 1, LIST), I32),
            vm((LIST, 128), F32),
            vm((2, NZ * HA, 128), F32),
            vm((2, NZ * HA, 128), F32),
            vm((2, NZ * RA, 128), F32),
            vm((2, NZ * RA, 128), F32),
            vm((NZ * RA, 128), F32),
            vm((2, HA, 128), F32),
            vm((3, 2, RA, 128), F32),
            vm((NX * RB, 128), F32),
            vm((NX, 2, HB, 128), F32),
            vm((3, NX, 2, RB, 128), F32),
            vm((3, NX, 2, RB, 128), F32),
            vm((NX * RB, 128), F32),
            vm((3, RB, 128), F32),
            vm((NY, LIST, 128), F32),
            vm((LIST, 128), F32),
            vm((COLS, NY * COLS), F32),
            vm((8, 8, NY * COLS), F32),
            vm((8, 8, NY * COLS), F32),
            vm((8, 8, NY * COLS), F32),
            dma((8,)),
            dma((3,)),
            dma((8,)),
            dma((8,)),
            dma,
            dma,
            dma((2,)),
            dma((2,)),
            dma((MESSAGES,)),
            dma((MESSAGES,)),
            dma((3,)),
            dma((3,)),
        ],
        compiler_params=pltpu.CompilerParams(
            collective_id=0, has_side_effects=True, vmem_limit_bytes=40 << 20
        ),
    )(*(pltpu.with_memory_space_constraint(v, pltpu.HBM) for v in operands))
    return both[:COLS], both[COLS:] * (1.0 / (LIST * 2 * CHIPS * 2))


def solution(mesh):
    placed = (P("cols", "rows"), P("rows"), P("rows"))
    return jax.shard_map(
        on_device,
        mesh=mesh,
        in_specs=placed,
        out_specs=(P("cols", "rows"), P("cols", None)),
        check_vma=False,
    )
```

```python
import jax
import jax.numpy as jnp
from jax import lax
from jax.experimental import pallas as pl
from jax.experimental.pallas import tpu as pltpu
from jax.sharding import PartitionSpec as P

MESH = pl.DeviceIdType.MESH
F32, BF16, I32 = jnp.float32, jnp.bfloat16, jnp.int32

NX, NZ, NY = 4, 8, 4
CHIPS = NX * NZ
COLS, ROWS = 64, 8192
KEEP = 4
LIST = CHIPS * KEEP
RA = 80
RB = LIST - RA
A_HALF = (-(-RA // 16) * 8, RA - -(-RA // 16) * 8)
B_HALF = (-(-RB // 16) * 8, RB - -(-RB // 16) * 8)
A_FROM, B_FROM = (0, A_HALF[0]), (0, B_HALF[0])
Z_ORDER = (4, 3, -3, 2, -2, 1, -1, 0)
Z_GROUPS = ((0, 1), (1, 2), (3, 2), (5, 2), (7, 1))
F_GROUPS = ((0, 1), (1, 2), (3, 5))
X_ORDER = (2, 1, -1, 0)


def hadamard_rows(copies):
    shape = (128, 128 * copies)
    parity = lax.broadcasted_iota(I32, shape, 0) & lax.broadcasted_iota(I32, shape, 1) & 127
    for shift in (4, 2, 1):
        parity = parity ^ (parity >> shift)
    return (1 - 2 * (parity & 1)).astype(F32).astype(BF16)


def butterflies(parts):
    for stride in (1, 2, 4):
        done = list(parts)
        for i in range(8):
            if not i & stride:
                done[i] = parts[i] + parts[i | stride]
                done[i | stride] = parts[i] - parts[i | stride]
        parts = done
    return parts


def kernel(
    m_ref, s_ref, id_ref, out_ref,
    x_v, xp_v, s_v, sp_v, y_v, t_v, id_v, cls_v, idr_v, ids_v, ids_s, sg_v,
    afs, afr, ans, anr, a_sum, a4r, azr,
    b4s, b4r, bs, br, b_sum, bxr,
    f_v, fp_v, p_v, g1r, g2r, g3r,
    lx_sem, sm_sem, xs_sem, xr_sem, ps_sem, pr_sem, is_sem, ir_sem, rs_sem, rr_sem,
    gs_sem, gr_sem, far_sem,
):
    me, y = lax.axis_index("rows"), lax.axis_index("cols")
    core, chip = me % 2, me // 2
    x, z = chip % NX, chip // NX
    corner = x * 2 + core

    def at(x_to, z_to, core_to):
        return {"rows": (lax.rem(z_to + NZ, NZ) * NX + lax.rem(x_to + NX, NX)) * 2 + core_to}

    partner = at(x, z, 1 - core)

    def remote(src, dst, send, recv, device):
        return pltpu.make_async_remote_copy(
            src_ref=src, dst_ref=dst, send_sem=send, recv_sem=recv, device_id=device, device_id_type=MESH
        )

    barrier = pltpu.get_barrier_semaphore()
    corners = []
    for o in range(1, 8):
        to = lax.rem(corner + o, 8)
        corners.append((to, at(to // 2, z, lax.rem(to, 2))))
    heights = [at(x, z + o, core) for o in range(1, NZ)]
    columns = [{"cols": lax.rem(y + o, NY)} for o in range(1, NY)]
    close = [at(x, z + o, core) for o in (1, 2, -1, -2)]
    for device in [device for _, device in corners] + close + columns:
        pl.semaphore_signal(barrier, inc=1, device_id=device, device_id_type=MESH)

    id_copy = pltpu.make_async_copy(id_ref, id_v, sm_sem.at[0])
    sign_copy = pltpu.make_async_copy(s_ref, s_v, sm_sem.at[1])
    id_copy.start()
    sign_copy.start()

    def own_copy(q):
        piece = pl.ds(pl.multiple_of(q * 1024, 1024), 1024)
        return pltpu.make_async_copy(m_ref.at[:, piece], x_v.at[q], lx_sem.at[q])

    for q in range(8):
        own_copy(q).start()

    id_copy.wait()
    row = id_v[...] & (ROWS - 1)
    place = ((row >> 7) & 1) * (ROWS // 2) + (row >> 8) * 128 + (row & 127)
    place = jnp.concatenate([place, jnp.zeros((6, 128), I32)], 0)
    lane = lax.broadcasted_iota(I32, (8, 128), 1)
    for c in range(2):
        packed = place if c == 0 else pltpu.roll(place, 128 - KEEP, 1)
        for i in range(4):
            packed = jnp.where((lane >> (2 + i)) & 1 == 1, pltpu.roll(packed, 128 - (KEEP << i), 1), packed)
        second = pltpu.roll(packed, 64, 1)
        cls_v[c] = jnp.where(lane[0:1] < 64, packed[0:1], second[1:2])

    pl.semaphore_wait(barrier, len(corners) + len(close) + len(columns))
    for o in (2, -2):
        pl.semaphore_signal(far_sem, inc=1, device_id=at(x, z + o, core), device_id_type=MESH)

    sign_out = remote(s_ref, sp_v, ps_sem, pr_sem, partner)
    sign_out.start()

    def pair_copy(q):
        piece = pl.ds(pl.multiple_of(q * 1024, 1024), 1024)
        return remote(m_ref.at[:, piece], xp_v.at[q], xs_sem.at[q], xr_sem.at[q], partner)

    pair_copy(0).start()

    def wait_all(ref, slots, sem):
        piece = ref.at[pl.ds(0, slots)]
        pltpu.make_async_copy(piece, piece, sem).wait()

    for to, device in corners:
        remote(cls_v.at[lax.rem(to, 2)], idr_v.at[corner], is_sem.at[0], ir_sem.at[0], device).start()
    idr_v[corner] = cls_v[core]
    for q in range(1, 8):
        pair_copy(q).start()

    def lists_along_z():
        pl.semaphore_wait(far_sem, 2)
        wait_all(idr_v, 7, ir_sem.at[0])
        for n in range(NX):
            ids_v[z * NX + n] = idr_v[2 * n] | ((idr_v[2 * n + 1] ^ (ROWS // 2)) << 16)
        four = ids_v.at[pl.ds(z * NX, NX)]
        for device in heights:
            remote(four, four, is_sem.at[1], ir_sem.at[1], device).start()

    block = lax.broadcasted_iota(I32, (LIST, 128), 0) // KEEP
    parity = block & chip
    for shift in (4, 2, 1):
        parity = parity ^ (parity >> shift)
    sg_v[...] = (1 - 2 * (parity & 1)).astype(F32)

    had = hadamard_rows(2)
    flip = (1 - 2 * core).astype(F32)
    sign_copy.wait()
    sign_out.wait_recv()

    with jax.named_scope("local transform"):

        def chunk(q, _):
            own_copy(q).wait()
            pair_copy(q).wait_recv()
            own_sign = s_v[pl.ds(pl.multiple_of(q * 8, 8), 8), :].astype(F32) * flip
            far_sign = sp_v[pl.ds(pl.multiple_of(q * 8, 8), 8), :].astype(F32)
            parts = []
            for i in range(8):
                lanes = slice(i * 128, (i + 1) * 128)
                parts.append(x_v[q, :, lanes] * own_sign[i : i + 1] + xp_v[q, :, lanes] * far_sign[i : i + 1])
            parts = butterflies(parts)
            for p in range(4):
                two = jnp.concatenate([parts[2 * p], parts[2 * p + 1]], 0)
                high = two.astype(BF16)
                low = (two - high.astype(F32)).astype(BF16)
                y_v[q, p] = lax.dot_general(
                    had, jnp.concatenate([high, low], 1), (((1,), (1,)), ((), ())), preferred_element_type=F32
                )
            return 0

        lax.fori_loop(0, 4, chunk, 0)
        lists_along_z()
        lax.fori_loop(4, 8, chunk, 0)

    with jax.named_scope("across chunks"):

        def across(i, _):
            p = i // 4
            for t in range(4):
                row = pl.multiple_of((i % 4) * 32 + t * 8, 8)
                parts = butterflies([y_v[q, p, pl.ds(row, 8), :] for q in range(8)])
                for q in range(8):
                    to = pl.multiple_of(q * 512 + p * 128 + row, 8)
                    t_v[pl.ds(to, 8), :] = parts[q]
                    t_v[pl.ds(to + ROWS // 2, 8), :] = pltpu.roll(parts[q], 64, 1)
            return 0

        lax.fori_loop(0, 16, across, 0)
    wait_all(ids_v, 7 * NX, ir_sem.at[1])
    lists = pltpu.make_async_copy(ids_v, ids_s, sm_sem.at[2])
    lists.start()
    lists.wait()

    half = lax.broadcasted_iota(I32, (1, 128), 1) < 64

    def gather(dst, at_row, of, first, rows):
        unroll = rows if rows <= 48 else rows // 2
        for start in range(first, first + rows, unroll):
            got = []
            for j in range(start, start + unroll):
                if j == start or j % KEEP == 0:
                    sign = sg_v[j : j + 1, :]
                word = ids_s[of, 0, j]
                a = t_v[pl.ds(word & 0xFFFF, 1), :]
                b = t_v[pl.ds(word >> 16, 1), :]
                got.append(jnp.where(half, a, b) * sign)
            for u in range(unroll):
                dst[pl.ds(at_row + (start - first + u), 1), :] = got[u]

    count = [0]

    def send(src, dst, device):
        n = count[0]
        count[0] += 1
        copy = remote(src, dst, rs_sem.at[n], rr_sem.at[n], device)
        copy.start()
        return copy

    ups = (at(x, z + 1, core), at(x, z - 1, core))
    twos = (at(x, z + 2, core), at(x, z - 2, core))

    def chip_at(dx, dz):
        return lax.rem(z + dz + NZ, NZ) * NX + lax.rem(x + dx + NX, NX)

    def pick(values, n):
        value = jnp.int32(values[0])
        for k in range(1, len(values)):
            value = jnp.where(n == k, values[k], value)
        return value

    sides = (at(x + 1, z, core), at(x - 1, z, core))
    af, an, az = {}, {}, {}

    def a_far(g):
        place, width = F_GROUPS[g]

        def one(n, _):
            chip_to = chip_at(2, pick(Z_ORDER[place : place + width], n))
            for d in range(2):
                at_row = pl.multiple_of((place + n) * A_HALF[d], 8)
                gather(afs.at[d], at_row, chip_to, A_FROM[d], A_HALF[d])
            return 0

        lax.fori_loop(0, width, one, 0)
        for d in range(2):
            part = pl.ds(place * A_HALF[d], width * A_HALF[d])
            af[g, d] = send(afs.at[d, part], afr.at[d, part], sides[d])

    def a_near(place, last):
        def one(n, _):
            d = lax.rem(n, 2)
            k = n // 2
            at_row = pl.multiple_of(k * RA, RA)
            gather(ans.at[d], at_row, chip_at(1 - 2 * d, pick(Z_ORDER, k)), 0, RA)
            return 0

        lax.fori_loop(2 * place, 2 * last, one, 0)

    def a_x(g):
        place, width = Z_GROUPS[g]
        part = pl.ds(place * RA, width * RA)
        for d in range(2):
            for f in range(3):
                if F_GROUPS[f][0] == place:
                    af[f, d].wait_recv()
            for k in range(place, place + width):
                rows = pl.ds(k * RA + A_FROM[d], A_HALF[d])
                ans[d, rows, :] = ans[d, rows, :] + afr[d, k * A_HALF[d] : (k + 1) * A_HALF[d], :]
            an[g, d] = send(ans.at[d, part], anr.at[d, part], sides[d])

    def a_own():
        def one(n, _):
            gather(a_sum, pl.multiple_of(n * RA, RA), chip_at(0, pick(Z_ORDER, n)), 0, RA)
            return 0

        lax.fori_loop(0, NZ, one, 0)

    def a_add(g):
        place, width = Z_GROUPS[g]
        an[g, 0].wait_recv()
        an[g, 1].wait_recv()
        part = slice(place * RA, (place + width) * RA)
        a_sum[part, :] = a_sum[part, :] + (anr[0, part, :] + anr[1, part, :])

    def a_z(step):
        for d in range(2):
            if step == 4:
                az[4, d] = send(a_sum.at[pl.ds(A_FROM[d], A_HALF[d])], a4r.at[d, pl.ds(0, A_HALF[d])], twos[d])
                continue
            at_row = (7 - 2 * step + d) * RA
            if step == 2:
                az[4, d].wait_recv()
                part = pl.ds(at_row + A_FROM[d], A_HALF[d])
                a_sum[part, :] = a_sum[part, :] + a4r[d, : A_HALF[d], :]
                az[3, d].wait_recv()
                part = pl.ds(at_row, RA)
                a_sum[part, :] = a_sum[part, :] + azr[2, d]
            to = twos[d] if step == 2 else ups[d]
            az[step, d] = send(a_sum.at[pl.ds(at_row, RA)], azr.at[step - 1, d], to)

    b4, bz, bx = {}, {}, {}

    def b_far():
        def one(h, _):
            gather(b4s, pl.multiple_of(h * RB, RB), chip_at(pick(X_ORDER, h), 4), RA, RB)
            return 0

        lax.fori_loop(0, NX, one, 0)
        for h in range(NX):
            for d in range(2):
                src = b4s.at[pl.ds(h * RB + B_FROM[d], B_HALF[d])]
                b4[h, d] = send(src, b4r.at[h, d, pl.ds(0, B_HALF[d])], twos[d])

    def b_own(step, first, last):
        def one(n, _):
            d = lax.rem(n, 2)
            h = n // 2
            dst = bs.at[step - 1, h, d]
            gather(dst, 0, chip_at(pick(X_ORDER, h), step - 2 * step * d), RA, RB)
            return 0

        lax.fori_loop(2 * first, 2 * last, one, 0)

    def b_z(step, h):
        for d in range(2):
            src = bs.at[step - 1, h, d]
            if step == 2:
                b4[h, d].wait_recv()
                part = pl.ds(B_FROM[d], B_HALF[d])
                src[part, :] = src[part, :] + b4r[h, d, : B_HALF[d], :]
            if step < 3:
                bz[step + 1, h, d].wait_recv()
                src[...] = src[...] + br[step, h, d]
            bz[step, h, d] = send(src, br.at[step - 1, h, d], ups[d])

    def b_home():
        def one(h, _):
            gather(b_sum, pl.multiple_of(h * RB, RB), chip_at(pick(X_ORDER, h), 0), RA, RB)
            return 0

        lax.fori_loop(0, NX, one, 0)

    def b_x(h):
        part = pl.ds(h * RB, RB)
        bz[1, h, 0].wait_recv()
        bz[1, h, 1].wait_recv()
        b_sum[part, :] = b_sum[part, :] + (br[0, h, 0] + br[0, h, 1])
        if X_ORDER[h]:
            bx[h] = send(b_sum.at[part], bxr.at[h], at(x + X_ORDER[h], z, core))

    scale = 1.0 / float(ROWS * CHIPS * 2) ** 0.5
    spread = {}

    def finish(first, rows, total):
        f_v[y, pl.ds(first, rows), :] = total * scale
        src = f_v.at[y, pl.ds(first, rows)]
        for o in range(1, NY):
            spread[first, o] = send(src, src, columns[o - 1])
        spread[first, 0] = send(src, fp_v.at[pl.ds(first, rows)], partner)

    def a_finish():
        total = a_sum[7 * RA : 8 * RA, :]
        for step in (1, 2):
            az[step, 0].wait_recv()
            az[step, 1].wait_recv()
            total = total + (azr[step - 1, 0] + azr[step - 1, 1])
        finish(0, RA, total)

    def b_finish():
        total = b_sum[3 * RB : 4 * RB, :]
        for h in range(3):
            bx[h].wait_recv()
            total = total + bxr[h]
        finish(RA, RB, total)

    with jax.named_scope("reduce"):
        b_far()
        a_far(0)
        a_far(1)
        b_own(3, 0, 4)
        b_z(3, 0)
        b_z(3, 1)
        b_z(3, 2)
        b_z(3, 3)
        a_far(2)
        a_near(0, 3)
        b_own(2, 0, 4)
        a_x(0)
        b_z(2, 0)
        b_z(2, 1)
        a_x(1)
        b_z(2, 2)
        b_z(2, 3)
        a_near(3, 8)
        a_x(2)
        a_x(3)
        a_x(4)
        b_own(1, 0, 4)
        b_home()
        a_own()
        a_add(0)
        a_z(4)
        b_z(1, 0)
        b_z(1, 1)
        b_z(1, 2)
        b_z(1, 3)
        a_add(1)
        a_z(3)
        a_add(2)
        b_x(0)
        b_x(1)
        b_x(2)
        a_z(2)
        a_add(3)
        a_z(1)
        b_x(3)
        a_add(4)
        b_finish()
        a_finish()

    def product(first, rows, before):
        for o in range(1, NY):
            spread[first, o].wait_recv()
        part = pl.ds(first, rows)
        mine_t = f_v[y, part, :].T
        for c in range(NY):
            whole = jnp.dot(mine_t, f_v[c, part, :], precision=lax.Precision.HIGHEST, preferred_element_type=F32)
            lanes = slice(c * COLS, (c + 1) * COLS)
            added = whole[:COLS, :COLS] + whole[COLS:, COLS:]
            p_v[:, lanes] = p_v[:, lanes] + added if before else added

    with jax.named_scope("gram product"):
        product(RA, RB, False)
        product(0, RA, True)

    def corner_copy(src_of, dst, n):
        return [remote(src_of(to), dst, gs_sem.at[n], gr_sem.at[n], device) for to, device in corners]

    def rows_of(n):
        return pl.ds(pl.multiple_of(n * 8, 8), 8)

    def all_seven(ref, n, sems=gr_sem):
        seven = ref.at[pl.ds(0, 7)]
        pltpu.make_async_copy(seven, seven, sems.at[n]).wait()

    with jax.named_scope("gram rows"):
        first = corner_copy(lambda to: p_v.at[rows_of(to)], g1r.at[corner], 0)
        for copy in first:
            copy.start()
        g1r[corner] = p_v[rows_of(corner), :]
    with jax.named_scope("drain"):
        sign_out.wait_send()

        def pair_done(q, _):
            pair_copy(q).wait_send()
            return 0

        lax.fori_loop(0, 8, pair_done, 0)

        wait_all(idr_v, 7, is_sem.at[0])
        wait_all(ids_v, 7 * NX, is_sem.at[1])
        for group in (af, an, az, b4, bz, bx):
            for copy in group.values():
                copy.wait_send()
    with jax.named_scope("sketch out"):
        for part in (RA, 0):
            spread[part, 0].wait_recv()
        mine = f_v[y]
        other = fp_v[...]
        even = jnp.where(core == 0, mine, other).reshape(16, 8, 128)
        odd = jnp.where(core == 0, other, mine).reshape(16, 8, 128)
        upper = lax.broadcasted_iota(I32, (16, 8, 128), 1) < 4
        one = jnp.where(upper, even, pltpu.roll(odd, 4, 1))
        two = jnp.where(upper, pltpu.roll(even, 4, 1), odd)
        whole = jnp.stack([one, two], 1).reshape(256, 128).T
        out_ref[:COLS, :] = jnp.where(core == 0, whole[:COLS], whole[COLS:])
    with jax.named_scope("gram along z"):
        all_seven(g1r, 0)
        g2r[z] = jnp.sum(g1r[...], 0)
        second = []
        for device in heights:
            second.append(remote(g2r.at[z], g2r.at[z], gs_sem.at[1], gr_sem.at[1], device))
            second[-1].start()
        all_seven(g2r, 1)
    with jax.named_scope("gram out"):
        g3r[corner] = jnp.sum(g2r[...], 0)
        third = corner_copy(lambda to: g3r.at[corner], g3r.at[corner], 2)
        for copy in third:
            copy.start()
        all_seven(g3r, 2)
        out_ref[COLS:, :] = g3r[...].reshape(COLS, NY * COLS)

    for copy in spread.values():
        copy.wait_send()
    for n in range(3):
        all_seven(g1r, n, gs_sem)


MESSAGES = 6 + 10 + 8 + 8 + 24 + 3 + 8


def on_device(matrix_t, signs, sample_ids):
    vm = pltpu.VMEM
    dma = pltpu.SemaphoreType.DMA
    vmem_spec = pl.BlockSpec(memory_space=pltpu.VMEM)
    operands = matrix_t, signs.reshape(64, 128), sample_ids.reshape(2, 128)
    both = pl.pallas_call(
        kernel,
        name="sketch_gram",
        out_shape=jax.ShapeDtypeStruct((2 * COLS, NY * COLS), F32),
        in_specs=[pl.BlockSpec(memory_space=pl.ANY)] * 3,
        out_specs=vmem_spec,
        scratch_shapes=[
            vm((8, COLS, 1024), F32),
            vm((8, COLS, 1024), F32),
            vm((64, 128), I32),
            vm((64, 128), I32),
            vm((8, 4, 128, 128), F32),
            vm((ROWS, 128), F32),
            vm((2, 128), I32),
            vm((2, 1, LIST), I32),
            vm((8, 1, LIST), I32),
            vm((CHIPS, 1, LIST), I32),
            pltpu.SMEM((CHIPS, 1, LIST), I32),
            vm((LIST, 128), F32),
            vm((2, NZ * A_HALF[0], 128), F32),
            vm((2, NZ * A_HALF[0], 128), F32),
            vm((2, NZ * RA, 128), F32),
            vm((2, NZ * RA, 128), F32),
            vm((NZ * RA, 128), F32),
            vm((2, A_HALF[0], 128), F32),
            vm((3, 2, RA, 128), F32),
            vm((NX * RB, 128), F32),
            vm((NX, 2, B_HALF[0], 128), F32),
            vm((3, NX, 2, RB, 128), F32),
            vm((3, NX, 2, RB, 128), F32),
            vm((NX * RB, 128), F32),
            vm((3, RB, 128), F32),
            vm((NY, LIST, 128), F32),
            vm((LIST, 128), F32),
            vm((COLS, NY * COLS), F32),
            vm((8, 8, NY * COLS), F32),
            vm((8, 8, NY * COLS), F32),
            vm((8, 8, NY * COLS), F32),
            dma((8,)),
            dma((3,)),
            dma((8,)),
            dma((8,)),
            dma,
            dma,
            dma((2,)),
            dma((2,)),
            dma((MESSAGES,)),
            dma((MESSAGES,)),
            dma((3,)),
            dma((3,)),
            pltpu.SemaphoreType.REGULAR,
        ],
        compiler_params=pltpu.CompilerParams(
            collective_id=0, has_side_effects=True, vmem_limit_bytes=40 << 20
        ),
    )(*(pltpu.with_memory_space_constraint(v, pltpu.HBM) for v in operands))
    return both[:COLS], both[COLS:] * (1.0 / (LIST * 2 * CHIPS * 2))


def solution(mesh):
    placed = (P("cols", "rows"), P("rows"), P("rows"))
    return jax.shard_map(
        on_device,
        mesh=mesh,
        in_specs=placed,
        out_specs=(P("cols", "rows"), P("cols", None)),
        check_vma=False,
    )
```

```python
import jax
import jax.numpy as jnp
from jax import lax
from jax.experimental import pallas as pl
from jax.experimental.pallas import tpu as pltpu
from jax.sharding import PartitionSpec as P

MESH = pl.DeviceIdType.MESH
F32, BF16, I32 = jnp.float32, jnp.bfloat16, jnp.int32

NX, NZ, NY = 4, 8, 4
CHIPS = NX * NZ
COLS, ROWS = 64, 8192
KEEP = 4
LIST = CHIPS * KEEP
RA = 80
RB = LIST - RA
A_HALF = (-(-RA // 16) * 8, RA - -(-RA // 16) * 8)
B_HALF = (-(-RB // 16) * 8, RB - -(-RB // 16) * 8)
A_FROM, B_FROM = (0, A_HALF[0]), (0, B_HALF[0])
Z_ORDER = (4, 3, -3, 2, -2, 1, -1, 0)
Z_GROUPS = ((0, 1), (1, 2), (3, 2), (5, 2), (7, 1))
F_GROUPS = ((0, 1), (1, 2), (3, 5))
X_ORDER = (2, 1, -1, 0)


def hadamard_rows(copies):
    shape = (128, 128 * copies)
    parity = lax.broadcasted_iota(I32, shape, 0) & lax.broadcasted_iota(I32, shape, 1) & 127
    for shift in (4, 2, 1):
        parity = parity ^ (parity >> shift)
    return (1 - 2 * (parity & 1)).astype(F32).astype(BF16)


def butterflies(parts):
    for stride in (1, 2, 4):
        done = list(parts)
        for i in range(8):
            if not i & stride:
                done[i] = parts[i] + parts[i | stride]
                done[i | stride] = parts[i] - parts[i | stride]
        parts = done
    return parts


def kernel(
    m_ref, s_ref, id_ref, out_ref,
    x_v, xp_v, s_v, sp_v, y_v, t_v, id_v, cls_v, idr_v, ids_v, ids_s, sg_v,
    afs, afr, ans, anr, a_sum, a4r, azr,
    b4s, b4r, bs, br, b_sum, bxr,
    f_v, fp_v, p_v, g1r, g2r, g3r,
    lx_sem, sm_sem, xs_sem, xr_sem, ps_sem, pr_sem, is_sem, ir_sem, rs_sem, rr_sem,
    gs_sem, gr_sem, far_sem,
):
    me, y = lax.axis_index("rows"), lax.axis_index("cols")
    core, chip = me % 2, me // 2
    x, z = chip % NX, chip // NX
    corner = x * 2 + core

    def at(x_to, z_to, core_to):
        return {"rows": (lax.rem(z_to + NZ, NZ) * NX + lax.rem(x_to + NX, NX)) * 2 + core_to}

    partner = at(x, z, 1 - core)

    def remote(src, dst, send, recv, device):
        return pltpu.make_async_remote_copy(
            src_ref=src, dst_ref=dst, send_sem=send, recv_sem=recv, device_id=device, device_id_type=MESH
        )

    barrier = pltpu.get_barrier_semaphore()
    corners = []
    for o in range(1, 8):
        to = lax.rem(corner + o, 8)
        corners.append((to, at(to // 2, z, lax.rem(to, 2))))
    heights = [at(x, z + o, core) for o in range(1, NZ)]
    columns = [{"cols": lax.rem(y + o, NY)} for o in range(1, NY)]
    close = [at(x, z + o, core) for o in (1, 2, -1, -2)]
    for device in [device for _, device in corners] + close + columns:
        pl.semaphore_signal(barrier, inc=1, device_id=device, device_id_type=MESH)

    id_copy = pltpu.make_async_copy(id_ref, id_v, sm_sem.at[0])
    sign_copy = pltpu.make_async_copy(s_ref, s_v, sm_sem.at[1])
    id_copy.start()
    sign_copy.start()

    def own_copy(q):
        piece = pl.ds(pl.multiple_of(q * 1024, 1024), 1024)
        return pltpu.make_async_copy(m_ref.at[:, piece], x_v.at[q], lx_sem.at[q])

    for q in range(8):
        own_copy(q).start()

    id_copy.wait()
    row = id_v[...] & (ROWS - 1)
    place = ((row >> 7) & 1) * (ROWS // 2) + (row >> 8) * 128 + (row & 127)
    place = jnp.concatenate([place, jnp.zeros((6, 128), I32)], 0)
    lane = lax.broadcasted_iota(I32, (8, 128), 1)
    for c in range(2):
        packed = place if c == 0 else pltpu.roll(place, 128 - KEEP, 1)
        for i in range(4):
            packed = jnp.where((lane >> (2 + i)) & 1 == 1, pltpu.roll(packed, 128 - (KEEP << i), 1), packed)
        second = pltpu.roll(packed, 64, 1)
        cls_v[c] = jnp.where(lane[0:1] < 64, packed[0:1], second[1:2])

    pl.semaphore_wait(barrier, len(corners) + len(close) + len(columns))
    for o in (2, -2):
        pl.semaphore_signal(far_sem, inc=1, device_id=at(x, z + o, core), device_id_type=MESH)

    for to, device in corners:
        remote(cls_v.at[lax.rem(to, 2)], idr_v.at[corner], is_sem.at[0], ir_sem.at[0], device).start()
    idr_v[corner] = cls_v[core]

    sign_out = remote(s_ref, sp_v, ps_sem, pr_sem, partner)
    sign_out.start()

    def pair_copy(q):
        piece = pl.ds(pl.multiple_of(q * 1024, 1024), 1024)
        return remote(m_ref.at[:, piece], xp_v.at[q], xs_sem.at[q], xr_sem.at[q], partner)

    for q in range(8):
        pair_copy(q).start()

    def wait_all(ref, slots, sem):
        piece = ref.at[pl.ds(0, slots)]
        pltpu.make_async_copy(piece, piece, sem).wait()

    def into_smem(level):
        four = pl.ds(level * NX, NX)
        return pltpu.make_async_copy(ids_v.at[four], ids_s.at[four], sm_sem.at[2])

    def lists_along_z():
        pl.semaphore_wait(far_sem, 2)
        wait_all(idr_v, 7, ir_sem.at[0])
        for n in range(NX):
            ids_v[z * NX + n] = idr_v[2 * n] | ((idr_v[2 * n + 1] ^ (ROWS // 2)) << 16)
        four = ids_v.at[pl.ds(z * NX, NX)]
        for o in (4, 3, 5, 2, 6, 1, 7):
            remote(four, four, is_sem.at[1], ir_sem.at[o], heights[o - 1]).start()
        into_smem(z).start()

    block = lax.broadcasted_iota(I32, (LIST, 128), 0) // KEEP
    parity = block & chip
    for shift in (4, 2, 1):
        parity = parity ^ (parity >> shift)
    sg_v[...] = (1 - 2 * (parity & 1)).astype(F32)

    had = hadamard_rows(2)
    flip = (1 - 2 * core).astype(F32)
    sign_copy.wait()
    sign_out.wait_recv()

    with jax.named_scope("local transform"):

        def chunk(q, _):
            own_copy(q).wait()
            pair_copy(q).wait_recv()
            own_sign = s_v[pl.ds(pl.multiple_of(q * 8, 8), 8), :].astype(F32) * flip
            far_sign = sp_v[pl.ds(pl.multiple_of(q * 8, 8), 8), :].astype(F32)
            parts = []
            for i in range(8):
                lanes = slice(i * 128, (i + 1) * 128)
                parts.append(x_v[q, :, lanes] * own_sign[i : i + 1] + xp_v[q, :, lanes] * far_sign[i : i + 1])
            parts = butterflies(parts)
            for p in range(4):
                two = jnp.concatenate([parts[2 * p], parts[2 * p + 1]], 0)
                high = two.astype(BF16)
                low = (two - high.astype(F32)).astype(BF16)
                y_v[q, p] = lax.dot_general(
                    had, jnp.concatenate([high, low], 1), (((1,), (1,)), ((), ())), preferred_element_type=F32
                )
            return 0

        lax.fori_loop(0, 4, chunk, 0)
        lists_along_z()
        lax.fori_loop(4, 8, chunk, 0)

    with jax.named_scope("across chunks"):

        def across(i, _):
            p = i // 4
            for t in range(4):
                row = pl.multiple_of((i % 4) * 32 + t * 8, 8)
                parts = butterflies([y_v[q, p, pl.ds(row, 8), :] for q in range(8)])
                for q in range(8):
                    to = pl.multiple_of(q * 512 + p * 128 + row, 8)
                    t_v[pl.ds(to, 8), :] = parts[q]
                    t_v[pl.ds(to + ROWS // 2, 8), :] = pltpu.roll(parts[q], 64, 1)
            return 0

        lax.fori_loop(0, 16, across, 0)
    for o in (1, 7, 2, 6, 3, 5, 4):
        level = lax.rem(z + NZ - o, NZ)
        four = ids_v.at[pl.ds(level * NX, NX)]
        remote(four, four, is_sem.at[1], ir_sem.at[o], heights[o - 1]).wait_recv()
        into_smem(level).start()
    pltpu.make_async_copy(ids_v, ids_s, sm_sem.at[2]).wait()

    half = lax.broadcasted_iota(I32, (1, 128), 1) < 64

    def gather(dst, at_row, of, first, rows):
        unroll = rows if rows <= 48 else rows // 2
        for start in range(first, first + rows, unroll):
            got = []
            for j in range(start, start + unroll):
                if j == start or j % KEEP == 0:
                    sign = sg_v[j : j + 1, :]
                word = ids_s[of, 0, j]
                a = t_v[pl.ds(word & 0xFFFF, 1), :]
                b = t_v[pl.ds(word >> 16, 1), :]
                got.append(jnp.where(half, a, b) * sign)
            for u in range(unroll):
                dst[pl.ds(at_row + (start - first + u), 1), :] = got[u]

    count = [0]

    def send(src, dst, device):
        n = count[0]
        count[0] += 1
        copy = remote(src, dst, rs_sem.at[n], rr_sem.at[n], device)
        copy.start()
        return copy

    ups = (at(x, z + 1, core), at(x, z - 1, core))
    twos = (at(x, z + 2, core), at(x, z - 2, core))

    def chip_at(dx, dz):
        return lax.rem(z + dz + NZ, NZ) * NX + lax.rem(x + dx + NX, NX)

    def pick(values, n):
        value = jnp.int32(values[0])
        for k in range(1, len(values)):
            value = jnp.where(n == k, values[k], value)
        return value

    sides = (at(x + 1, z, core), at(x - 1, z, core))
    af, an, az = {}, {}, {}

    def a_far(g):
        place, width = F_GROUPS[g]

        def one(n, _):
            chip_to = chip_at(2, pick(Z_ORDER[place : place + width], n))
            for d in range(2):
                at_row = pl.multiple_of((place + n) * A_HALF[d], 8)
                gather(afs.at[d], at_row, chip_to, A_FROM[d], A_HALF[d])
            return 0

        lax.fori_loop(0, width, one, 0)
        for d in range(2):
            part = pl.ds(place * A_HALF[d], width * A_HALF[d])
            af[g, d] = send(afs.at[d, part], afr.at[d, part], sides[d])

    def a_near(place, last):
        def one(n, _):
            d = lax.rem(n, 2)
            k = n // 2
            at_row = pl.multiple_of(k * RA, RA)
            gather(ans.at[d], at_row, chip_at(1 - 2 * d, pick(Z_ORDER, k)), 0, RA)
            return 0

        lax.fori_loop(2 * place, 2 * last, one, 0)

    def a_x(g):
        place, width = Z_GROUPS[g]
        part = pl.ds(place * RA, width * RA)
        for d in range(2):
            for f in range(3):
                if F_GROUPS[f][0] == place:
                    af[f, d].wait_recv()
            for k in range(place, place + width):
                rows = pl.ds(k * RA + A_FROM[d], A_HALF[d])
                ans[d, rows, :] = ans[d, rows, :] + afr[d, k * A_HALF[d] : (k + 1) * A_HALF[d], :]
            an[g, d] = send(ans.at[d, part], anr.at[d, part], sides[d])

    def a_own():
        def one(n, _):
            gather(a_sum, pl.multiple_of(n * RA, RA), chip_at(0, pick(Z_ORDER, n)), 0, RA)
            return 0

        lax.fori_loop(0, NZ, one, 0)

    def a_add(g):
        place, width = Z_GROUPS[g]
        an[g, 0].wait_recv()
        an[g, 1].wait_recv()
        part = slice(place * RA, (place + width) * RA)
        a_sum[part, :] = a_sum[part, :] + (anr[0, part, :] + anr[1, part, :])

    def a_z(step):
        for d in range(2):
            if step == 4:
                az[4, d] = send(a_sum.at[pl.ds(A_FROM[d], A_HALF[d])], a4r.at[d, pl.ds(0, A_HALF[d])], twos[d])
                continue
            at_row = (7 - 2 * step + d) * RA
            if step == 2:
                az[4, d].wait_recv()
                part = pl.ds(at_row + A_FROM[d], A_HALF[d])
                a_sum[part, :] = a_sum[part, :] + a4r[d, : A_HALF[d], :]
                az[3, d].wait_recv()
                part = pl.ds(at_row, RA)
                a_sum[part, :] = a_sum[part, :] + azr[2, d]
            to = twos[d] if step == 2 else ups[d]
            az[step, d] = send(a_sum.at[pl.ds(at_row, RA)], azr.at[step - 1, d], to)

    b4, bz, bx = {}, {}, {}

    def b_far():
        def one(h, _):
            gather(b4s, pl.multiple_of(h * RB, RB), chip_at(pick(X_ORDER, h), 4), RA, RB)
            return 0

        lax.fori_loop(0, NX, one, 0)
        for h in range(NX):
            for d in range(2):
                src = b4s.at[pl.ds(h * RB + B_FROM[d], B_HALF[d])]
                b4[h, d] = send(src, b4r.at[h, d, pl.ds(0, B_HALF[d])], twos[d])

    def b_own(step, first, last):
        def one(n, _):
            d = lax.rem(n, 2)
            h = n // 2
            dst = bs.at[step - 1, h, d]
            gather(dst, 0, chip_at(pick(X_ORDER, h), step - 2 * step * d), RA, RB)
            return 0

        lax.fori_loop(2 * first, 2 * last, one, 0)

    def b_z(step, h):
        for d in range(2):
            src = bs.at[step - 1, h, d]
            if step == 2:
                b4[h, d].wait_recv()
                part = pl.ds(B_FROM[d], B_HALF[d])
                src[part, :] = src[part, :] + b4r[h, d, : B_HALF[d], :]
            if step < 3:
                bz[step + 1, h, d].wait_recv()
                src[...] = src[...] + br[step, h, d]
            bz[step, h, d] = send(src, br.at[step - 1, h, d], ups[d])

    def b_home():
        def one(h, _):
            gather(b_sum, pl.multiple_of(h * RB, RB), chip_at(pick(X_ORDER, h), 0), RA, RB)
            return 0

        lax.fori_loop(0, NX, one, 0)

    def b_x(h):
        part = pl.ds(h * RB, RB)
        bz[1, h, 0].wait_recv()
        bz[1, h, 1].wait_recv()
        b_sum[part, :] = b_sum[part, :] + (br[0, h, 0] + br[0, h, 1])
        if X_ORDER[h]:
            bx[h] = send(b_sum.at[part], bxr.at[h], at(x + X_ORDER[h], z, core))

    scale = 1.0 / float(ROWS * CHIPS * 2) ** 0.5
    spread = {}

    def finish(first, rows, total):
        f_v[y, pl.ds(first, rows), :] = total * scale
        src = f_v.at[y, pl.ds(first, rows)]
        for o in range(1, NY):
            spread[first, o] = send(src, src, columns[o - 1])
        spread[first, 0] = send(src, fp_v.at[pl.ds(first, rows)], partner)

    def a_finish():
        total = a_sum[7 * RA : 8 * RA, :]
        for step in (1, 2):
            az[step, 0].wait_recv()
            az[step, 1].wait_recv()
            total = total + (azr[step - 1, 0] + azr[step - 1, 1])
        finish(0, RA, total)

    def b_finish():
        total = b_sum[3 * RB : 4 * RB, :]
        for h in range(3):
            bx[h].wait_recv()
            total = total + bxr[h]
        finish(RA, RB, total)

    with jax.named_scope("reduce"):
        b_far()
        a_far(0)
        a_far(1)
        b_own(3, 0, 4)
        b_z(3, 0)
        b_z(3, 1)
        b_z(3, 2)
        b_z(3, 3)
        a_far(2)
        a_near(0, 3)
        b_own(2, 0, 4)
        a_x(0)
        b_z(2, 0)
        b_z(2, 1)
        a_x(1)
        b_z(2, 2)
        b_z(2, 3)
        a_near(3, 8)
        a_x(2)
        a_x(3)
        a_x(4)
        b_own(1, 0, 4)
        b_home()
        a_own()
        a_add(0)
        a_z(4)
        b_z(1, 0)
        b_z(1, 1)
        b_z(1, 2)
        b_z(1, 3)
        a_add(1)
        a_z(3)
        a_add(2)
        b_x(0)
        b_x(1)
        b_x(2)
        a_z(2)
        a_add(3)
        a_z(1)
        b_x(3)
        a_add(4)
        b_finish()
        a_finish()

    def product(first, rows, before):
        for o in range(1, NY):
            spread[first, o].wait_recv()
        part = pl.ds(first, rows)
        mine_t = f_v[y, part, :].T
        for c in range(NY):
            whole = jnp.dot(mine_t, f_v[c, part, :], precision=lax.Precision.HIGHEST, preferred_element_type=F32)
            lanes = slice(c * COLS, (c + 1) * COLS)
            added = whole[:COLS, :COLS] + whole[COLS:, COLS:]
            p_v[:, lanes] = p_v[:, lanes] + added if before else added

    with jax.named_scope("gram product"):
        product(RA, RB, False)
        product(0, RA, True)

    def corner_copy(src_of, dst, n):
        return [remote(src_of(to), dst, gs_sem.at[n], gr_sem.at[n], device) for to, device in corners]

    def rows_of(n):
        return pl.ds(pl.multiple_of(n * 8, 8), 8)

    def all_seven(ref, n, sems=gr_sem):
        seven = ref.at[pl.ds(0, 7)]
        pltpu.make_async_copy(seven, seven, sems.at[n]).wait()

    with jax.named_scope("gram rows"):
        first = corner_copy(lambda to: p_v.at[rows_of(to)], g1r.at[corner], 0)
        for copy in first:
            copy.start()
        g1r[corner] = p_v[rows_of(corner), :]
    with jax.named_scope("drain"):
        sign_out.wait_send()

        def pair_done(q, _):
            pair_copy(q).wait_send()
            return 0

        lax.fori_loop(0, 8, pair_done, 0)

        wait_all(idr_v, 7, is_sem.at[0])
        wait_all(ids_v, 7 * NX, is_sem.at[1])
        for group in (af, an, az, b4, bz, bx):
            for copy in group.values():
                copy.wait_send()
    with jax.named_scope("sketch out"):
        for part in (RA, 0):
            spread[part, 0].wait_recv()
        mine = f_v[y]
        other = fp_v[...]
        even = jnp.where(core == 0, mine, other).reshape(16, 8, 128)
        odd = jnp.where(core == 0, other, mine).reshape(16, 8, 128)
        upper = lax.broadcasted_iota(I32, (16, 8, 128), 1) < 4
        one = jnp.where(upper, even, pltpu.roll(odd, 4, 1))
        two = jnp.where(upper, pltpu.roll(even, 4, 1), odd)
        whole = jnp.stack([one, two], 1).reshape(256, 128).T
        out_ref[:COLS, :] = jnp.where(core == 0, whole[:COLS], whole[COLS:])
    with jax.named_scope("gram along z"):
        all_seven(g1r, 0)
        g2r[z] = jnp.sum(g1r[...], 0)
        second = []
        for device in heights:
            second.append(remote(g2r.at[z], g2r.at[z], gs_sem.at[1], gr_sem.at[1], device))
            second[-1].start()
        all_seven(g2r, 1)
    with jax.named_scope("gram out"):
        g3r[corner] = jnp.sum(g2r[...], 0)
        third = corner_copy(lambda to: g3r.at[corner], g3r.at[corner], 2)
        for copy in third:
            copy.start()
        all_seven(g3r, 2)
        out_ref[COLS:, :] = g3r[...].reshape(COLS, NY * COLS)

    for copy in spread.values():
        copy.wait_send()
    for n in range(3):
        all_seven(g1r, n, gs_sem)


MESSAGES = 6 + 10 + 8 + 8 + 24 + 3 + 8


def on_device(matrix_t, signs, sample_ids):
    vm = pltpu.VMEM
    dma = pltpu.SemaphoreType.DMA
    vmem_spec = pl.BlockSpec(memory_space=pltpu.VMEM)
    operands = matrix_t, signs.reshape(64, 128), sample_ids.reshape(2, 128)
    both = pl.pallas_call(
        kernel,
        name="sketch_gram",
        out_shape=jax.ShapeDtypeStruct((2 * COLS, NY * COLS), F32),
        in_specs=[pl.BlockSpec(memory_space=pl.ANY)] * 3,
        out_specs=vmem_spec,
        scratch_shapes=[
            vm((8, COLS, 1024), F32),
            vm((8, COLS, 1024), F32),
            vm((64, 128), I32),
            vm((64, 128), I32),
            vm((8, 4, 128, 128), F32),
            vm((ROWS, 128), F32),
            vm((2, 128), I32),
            vm((2, 1, LIST), I32),
            vm((8, 1, LIST), I32),
            vm((CHIPS, 1, LIST), I32),
            pltpu.SMEM((CHIPS, 1, LIST), I32),
            vm((LIST, 128), F32),
            vm((2, NZ * A_HALF[0], 128), F32),
            vm((2, NZ * A_HALF[0], 128), F32),
            vm((2, NZ * RA, 128), F32),
            vm((2, NZ * RA, 128), F32),
            vm((NZ * RA, 128), F32),
            vm((2, A_HALF[0], 128), F32),
            vm((3, 2, RA, 128), F32),
            vm((NX * RB, 128), F32),
            vm((NX, 2, B_HALF[0], 128), F32),
            vm((3, NX, 2, RB, 128), F32),
            vm((3, NX, 2, RB, 128), F32),
            vm((NX * RB, 128), F32),
            vm((3, RB, 128), F32),
            vm((NY, LIST, 128), F32),
            vm((LIST, 128), F32),
            vm((COLS, NY * COLS), F32),
            vm((8, 8, NY * COLS), F32),
            vm((8, 8, NY * COLS), F32),
            vm((8, 8, NY * COLS), F32),
            dma((8,)),
            dma((3,)),
            dma((8,)),
            dma((8,)),
            dma,
            dma,
            dma((2,)),
            dma((8,)),
            dma((MESSAGES,)),
            dma((MESSAGES,)),
            dma((3,)),
            dma((3,)),
            pltpu.SemaphoreType.REGULAR,
        ],
        compiler_params=pltpu.CompilerParams(
            collective_id=0, has_side_effects=True, vmem_limit_bytes=40 << 20
        ),
    )(*(pltpu.with_memory_space_constraint(v, pltpu.HBM) for v in operands))
    return both[:COLS], both[COLS:] * (1.0 / (LIST * 2 * CHIPS * 2))


def solution(mesh):
    placed = (P("cols", "rows"), P("rows"), P("rows"))
    return jax.shard_map(
        on_device,
        mesh=mesh,
        in_specs=placed,
        out_specs=(P("cols", "rows"), P("cols", None)),
        check_vma=False,
    )
```
